32 devices in a mesh: bus: 8 (over z, y), tm: 4 (over x, core).
Axes of the slice: x: 2, y: 2, z: 4, core: 2. Of those that a mesh axis runs over, the one named last changes fastest.
Arguments:
- features: bfloat16 [1024, 64, 128], P('bus', 'tm'), may hold values from -6 to 6
- couplings: bfloat16 [16, 8, 64, 64], P('bus'), may hold values from -0.25 to 0.25
- neighbors: int32 [16, 8], P('bus'), may hold values from 0 to 15, as said below
- w_graph: bfloat16 [128, 128], replicated, may hold values from -0.5 to 0.5
- kernel_taps: bfloat16 [64, 128], replicated, may hold values from -0.3984375 to 0.3984375
- w_out: bfloat16 [128, 128], replicated, may hold values from -0.5 to 0.5
- cotangent: bfloat16 [1024, 64, 128], P('bus', 'tm'), may hold values from -6 to 6
Outputs:
- grad_features: bfloat16 [1024, 64, 128], P('bus', 'tm')
- grad_graph: float32 [128, 128], replicated
- grad_out: float32 [128, 128], replicated
- grad_taps: float32 [64, 128], replicated
The draws below stay inside these ranges and needn't reach their ends.
Inputs may be any that keep to these rules, and one draw needn't show every extreme that they name: neighbors[i, 0] = i. Counting 2 blocks to each index of bus, every entry of block i names a block of the same index, one of the last 1 block of the index before, or one of the first 1 block of the index after.
All inputs are finite; a program needn't handle non-finite values.
Results may differ from the reference program's by a relative error of at most 0.0067.
Values may be sent and summed in bfloat16 or wider, within the bound.
No kernel may reach another device: no remote copies, remote signals or barrier semaphores. Data moves between devices by JAX's collectives and lax.ppermute only.
A program may use at most 64 MiB of HBM per device.

```python
import math
import jax
import jax.numpy as jnp
from jax import lax

C = 128
BUSES_PER_BLOCK = 64
COUPLING_SLOTS = 8
BORDER_BLOCKS = 1
BLOCKS_PER_SHARD = 2
TOTAL_BLOCKS = 16
NB = 1024
TIME = 64


def draw_neighbors(key, part):
    block_ids = jnp.arange(TOTAL_BLOCKS, dtype=jnp.int32)
    owner = block_ids // BLOCKS_PER_SHARD
    slot_offsets = jax.random.randint(key, (TOTAL_BLOCKS, COUPLING_SLOTS - 1), -BORDER_BLOCKS, BLOCKS_PER_SHARD + BORDER_BLOCKS, dtype=jnp.int32)
    target = jnp.clip(owner[:, None] * BLOCKS_PER_SHARD + slot_offsets, 0, TOTAL_BLOCKS - 1)
    return jnp.concatenate([block_ids[:, None], target], axis=1).astype(jnp.int32)


def block_scale(key, shape, pieces, least, high):
    gain, own = 1.0, jax.random.fold_in(key, 6)
    for axis_at, parts in pieces:
        heights = jnp.exp(jax.random.uniform(jax.random.fold_in(own, axis_at), (parts,), jnp.float32, least / len(pieces), high / len(pieces)))
        gain = gain * jnp.repeat(heights, shape[axis_at] // parts).reshape([-1 if axis == axis_at else 1 for axis in range(len(shape))])
    return gain


def noise(own_key, shape, width, most, pieces=(), held_as=jnp.bfloat16):
    loudness = block_scale(own_key, shape, pieces, -0.22, 0.18) if pieces else 1.0
    values = jax.random.normal(own_key, shape, jnp.float32) * width * loudness
    return jnp.minimum(jnp.maximum(values, -most), most).astype(held_as)


def setup_inputs(seed: int = 0) -> dict:
    key_of = jax.random.split(jax.random.key(seed), 8)
    return {
        "features": noise(key_of[0], (NB, TIME, C), 1.0, 6.0, ((0, 8), (1, 4))),
        "couplings": noise(key_of[1], (TOTAL_BLOCKS, COUPLING_SLOTS, BUSES_PER_BLOCK, BUSES_PER_BLOCK), (BUSES_PER_BLOCK * COUPLING_SLOTS) ** -0.5, 0.25, ((0, 8),)),
        "neighbors": draw_neighbors(jax.random.fold_in(key_of[7], 71), 0),
        "w_graph": noise(key_of[3], (C, C), C ** -0.5, 0.5),
        "kernel_taps": noise(key_of[4], (TIME, C), 0.07, 0.3984375),
        "w_out": noise(key_of[5], (C, C), C ** -0.5, 0.5),
        "cotangent": noise(key_of[6], (NB, TIME, C), 1.0, 6.0, ((0, 8), (1, 4))),
    }


def rounded(values):
    return lax.optimization_barrier(values.astype(jnp.bfloat16)).astype(jnp.float32)

def toeplitz_table(kernel_taps):
    length = kernel_taps.shape[0]
    row_ids = jnp.arange(length, dtype=jnp.int32)
    lagged = row_ids[:, None] - row_ids[None, :]
    picked = jnp.take(kernel_taps.T, jnp.clip(lagged, 0, length - 1), axis=1)
    return jnp.where(lagged[None] >= 0, picked, jnp.zeros_like(picked))

def lag_sums(lag_table):
    channels = lag_table.shape[0]
    length = lag_table.shape[1]
    flipped = lag_table[:, :, ::-1]
    padded = jnp.pad(flipped, ((0, 0), (0, 0), (0, 1)))
    flat_view = padded.reshape(channels, length * (length + 1))
    window = flat_view[:, length - 1:length - 1 + length * length].reshape(channels, length, length)
    row_ids = jnp.arange(length, dtype=jnp.int32)
    lag_mask = row_ids[None, :, None] >= row_ids[None, None, :]
    return lax.optimization_barrier(jnp.sum(jnp.where(lag_mask, window, jnp.zeros_like(window)), axis=1)).T

def silu_slope(pre_act):
    sigmoid_val = jax.nn.sigmoid(pre_act)
    return sigmoid_val * (1.0 + pre_act * (1.0 - sigmoid_val))

def reference(features, couplings, neighbors, w_graph, kernel_taps, w_out, cotangent):
    flat_len = TIME * C
    blocks_in = features.reshape(TOTAL_BLOCKS, BUSES_PER_BLOCK, flat_len)

    def graph_one(block_index):
        gathered = blocks_in[neighbors[block_index]].astype(jnp.float32)
        return jnp.einsum('kab,kbn->an', couplings[block_index].astype(jnp.float32), gathered).astype(jnp.bfloat16)
    mixed_blocks = lax.map(graph_one, jnp.arange(TOTAL_BLOCKS, dtype=jnp.int32))
    lag_table = toeplitz_table(kernel_taps).astype(jnp.float32)
    graph_weight = w_graph.astype(jnp.float32)
    out_weight = w_out.astype(jnp.float32)
    cot_blocks = cotangent.reshape(TOTAL_BLOCKS, BUSES_PER_BLOCK, TIME, C)

    def pointwise(pair):
        mixed_one, cot_one = pair
        mixed_one = mixed_one.reshape(BUSES_PER_BLOCK, TIME, C).astype(jnp.float32)
        pre_act = jnp.einsum('btc,cd->btd', mixed_one, graph_weight)
        activated = rounded(jax.nn.silu(pre_act))
        convolved_rows = rounded(jnp.einsum('cts,bsc->btc', lag_table, activated))
        cot_float = cot_one.astype(jnp.float32)
        part_out = jnp.einsum('btc,btd->cd', convolved_rows, cot_float)
        grad_conv = rounded(jnp.einsum('btd,cd->btc', cot_float, out_weight))
        part_taps = lag_sums(jnp.einsum('btc,bsc->cts', grad_conv, activated))
        grad_act = rounded(jnp.einsum('cts,btc->bsc', lag_table, grad_conv))
        grad_pre = rounded(grad_act * silu_slope(pre_act))
        part_graph = jnp.einsum('btc,btd->cd', mixed_one, grad_pre)
        grad_mixed = jnp.einsum('btd,cd->btc', grad_pre, graph_weight).astype(jnp.bfloat16)
        return (grad_mixed.reshape(BUSES_PER_BLOCK, flat_len), part_graph, part_out, part_taps)
    grad_mixed, parts_graph, parts_out, parts_taps = lax.map(pointwise, (mixed_blocks, cot_blocks))

    def spread_one(total_sum, block_index):
        contrib = jnp.einsum('kab,an->kbn', couplings[block_index].astype(jnp.float32), grad_mixed[block_index].astype(jnp.float32))
        return (total_sum.at[neighbors[block_index]].add(contrib), None)
    start_sum = jnp.zeros((TOTAL_BLOCKS, BUSES_PER_BLOCK, flat_len), jnp.float32)
    total_sum, unused = lax.scan(spread_one, start_sum, jnp.arange(TOTAL_BLOCKS, dtype=jnp.int32))
    grad_features = (total_sum.reshape(NB, TIME, C) + cotangent.astype(jnp.float32)).astype(jnp.bfloat16)
    grad_scale = 1.0 / math.sqrt(NB * TIME)
    grad_graph = lax.optimization_barrier(jnp.sum(parts_graph, axis=0)) * grad_scale
    grad_out = lax.optimization_barrier(jnp.sum(parts_out, axis=0)) * grad_scale
    grad_taps = lax.optimization_barrier(jnp.sum(parts_taps, axis=0)) * grad_scale
    return (grad_features, grad_graph, grad_out, grad_taps)
```

```python
import math

import jax
import jax.numpy as jnp
from jax import lax
from jax.experimental import pallas as pl
from jax.experimental.pallas import tpu as pltpu
from jax.sharding import PartitionSpec as P

BF = jnp.bfloat16
F32 = jnp.float32
VMEM = pl.BlockSpec(memory_space=pltpu.VMEM)
LIMIT = 48 * 1024 * 1024


def call(body, outs, *args, scratch=(), flops=1 << 28):
    return pl.pallas_call(
        body,
        out_shape=[jax.ShapeDtypeStruct(shape, dtype) for shape, dtype in outs],
        in_specs=[VMEM] * len(args),
        out_specs=[VMEM] * len(outs),
        scratch_shapes=list(scratch),
        compiler_params=pltpu.CompilerParams(vmem_limit_bytes=LIMIT),
        cost_estimate=pl.CostEstimate(flops=flops, bytes_accessed=1 << 20, transcendentals=0),
    )(*args)


def dot(left, right, dims=((1,), (0,))):
    return lax.dot_general(left, right, (dims, ((), ())), preferred_element_type=F32)


def time_major(value):
    return jnp.swapaxes(value.astype(F32), 0, 1).astype(BF)


def split_body(feat_ref, cot_ref, own_ref, first_ref, last_ref, cot_out_ref):
    rows = feat_ref.shape[0]
    half = first_ref.shape[1]
    for start in range(0, rows, 16):
        part = time_major(feat_ref[start : start + 16])
        own_ref[:, start : start + 16] = part
        if start < half:
            first_ref[:, start : start + 16] = part
        if start >= rows - half:
            at = start - (rows - half)
            last_ref[:, at : at + 16] = part
        cot_out_ref[:, start : start + 16] = time_major(cot_ref[start : start + 16])


def conv_body(slot_ref, c0_ref, c1_ref, c2_ref, c3_ref, taps_ref, wout_ref, grad_ref, cross_ref, conv, lags):
    steps, rows, chans = c0_ref.shape
    total = taps_ref.shape[0]
    near, far = slot_ref[0], slot_ref[1]
    for at, ref in ((0, c0_ref), (near, c1_ref), (2, c2_ref), (far, c3_ref)):
        for s in range(0, steps, 4):
            block = ref[s : s + 4].reshape(4 * rows, chans)
            conv[at, s : s + 4] = (
                dot(block, wout_ref[...], ((1,), (1,))).astype(BF).reshape(4, rows, chans)
            )
        for s in range(0, steps, 2):
            cross_ref[at * (steps // 2) + s // 2, :, 0:rows] = ref[s].T
            cross_ref[at * (steps // 2) + s // 2, :, rows : 2 * rows] = ref[s + 1].T
    cross_ref[2 * steps :] = jnp.zeros_like(cross_ref[2 * steps :])
    lags[0:16] = jnp.zeros((16, 8, chans), F32)
    taps = taps_ref[...].astype(F32)
    for lag in range(total):
        lags[16 + lag] = jnp.broadcast_to(taps[lag : lag + 1], (8, chans))

    def tile(index, carry):
        where = pl.ds(pl.multiple_of(index * 16, 16), 16)
        sums = [[jnp.zeros((8, chans), F32)] * 2 for _ in range(steps)]
        for j in range(4):
            for t in range(steps):
                value = conv[j, t, where, :].astype(F32)
                for s in range(steps):
                    lag = j * steps + t - s
                    if lag < 0:
                        continue
                    tap = lags[16 + lag]
                    sums[s][0] += tap * value[:8]
                    sums[s][1] += tap * value[8:]
        for s in range(steps):
            grad_ref[s, where, :] = jnp.concatenate(sums[s], axis=0).astype(BF)
        return carry

    lax.fori_loop(0, rows // 16, tile, 0)


def main_body(
    own_ref, before_ref, after_ref, mix_ref, mixt_ref, wg_ref, grad_ref,
    act_ref, spread_ref, down_ref, up_ref, graph_ref,
):
    steps, rows, chans = own_ref.shape
    half = before_ref.shape[1]
    group = 4
    mix, mixt, wg = mix_ref[...], mixt_ref[...], wg_ref[...]
    graph = jnp.zeros((chans, chans), F32)
    for s in range(0, steps, group):
        ext = jnp.concatenate(
            [
                jnp.concatenate([before_ref[t], own_ref[t], after_ref[t]], axis=0)
                for t in range(s, s + group)
            ],
            axis=1,
        )
        mixed = dot(mix, ext).astype(BF)
        mixed = jnp.concatenate(
            [mixed[:, t * chans : (t + 1) * chans] for t in range(group)], axis=0
        )
        pre = dot(mixed, wg)
        gate = 1.0 / (1.0 + jnp.exp(-pre))
        act = pre * gate
        act_ref[s : s + group] = act.astype(BF).reshape(group, rows, chans)
        slope = gate * (1.0 + pre * (1.0 - gate))
        grad = grad_ref[s : s + group].reshape(group * rows, chans).astype(F32)
        grad_pre = (grad * slope).astype(BF)
        graph += dot(mixed, grad_pre, ((0,), (0,)))
        grad_mixed = dot(grad_pre, wg, ((1,), (1,))).astype(BF)
        grad_mixed = jnp.concatenate(
            [grad_mixed[t * rows : (t + 1) * rows] for t in range(group)], axis=1
        )
        spread = dot(mixt, grad_mixed)
        for t in range(group):
            part = spread[:, t * chans : (t + 1) * chans]
            down_ref[s + t] = part[:half].astype(BF)
            spread_ref[s + t] = part[half : half + rows]
            up_ref[s + t] = part[half + rows :].astype(BF)
    graph_ref[...] = graph


def lag_body(act_ref, cross_ref, taps_ref, wout_ref, out_ref, lag_ref, stack, acc_ref):
    steps, rows, chans = act_ref.shape
    pairs = cross_ref.shape[0] - steps // 2
    zero = jnp.zeros((rows, chans), BF)
    for i in range(steps // 2 + 1):
        s = 2 * i
        stack[i, 0:rows, 0:chans] = act_ref[s] if s < steps else zero
        stack[i, rows : 2 * rows, 0:chans] = act_ref[s + 1] if s < steps else zero
        stack[i, 0:rows, chans : 2 * chans] = act_ref[s - 1] if s > 0 else zero
        stack[i, rows : 2 * rows, chans : 2 * chans] = act_ref[s] if s < steps else zero
    acc_ref[...] = jnp.zeros_like(acc_ref)
    weight = wout_ref[...].astype(F32).T

    def group(index, carry):
        at = index * 2
        total = jnp.zeros((2 * rows, 2 * chans), F32)
        for i in range(steps // 2 + 1):
            left = cross_ref[pl.ds(at + i, 2)].reshape(2 * rows, 2 * rows)
            total += dot(left, stack[i])
        taps = taps_ref[pl.ds(pl.multiple_of(index * 8, 8), 8)]
        found = []
        acc = jnp.zeros((chans, chans), F32)
        for lag in range(4):
            part = total[(lag // 2) * rows : (lag // 2 + 1) * rows, (lag % 2) * chans : (lag % 2 + 1) * chans]
            acc += part * taps[lag : lag + 1]
            found.append(jnp.sum(part * weight, axis=0, keepdims=True))
        acc_ref[...] += acc
        lag_ref[pl.ds(pl.multiple_of(index * 8, 8), 8)] = jnp.concatenate(found + found, axis=0)
        return carry

    lax.fori_loop(0, pairs // 2, group, 0)
    out_ref[...] = acc_ref[...].T


def final_body(spread_ref, before_ref, after_ref, cot_ref, out_ref):
    rows = spread_ref.shape[1]
    half = before_ref.shape[1]
    for start in range(0, rows, 16):
        value = spread_ref[:, start : start + 16]
        if start < half:
            value = value + before_ref[:, start : start + 16].astype(F32)
        if start >= rows - half:
            at = start - (rows - half)
            value = value + after_ref[:, at : at + 16].astype(F32)
        part = jnp.swapaxes(value, 0, 1) + cot_ref[start : start + 16].astype(F32)
        out_ref[start : start + 16] = part.astype(BF)


def swap(value, axis, distance):
    size = lax.axis_size(axis)
    return lax.ppermute(value, axis, [(i, i ^ distance) for i in range(size)])


def reduce_all(value, bus, tm):
    side = lax.axis_index("tm") & 1
    halves = value.reshape(2, value.shape[0] // 2, value.shape[1])
    keep = lax.dynamic_index_in_dim(halves, side, 0, False)
    send = lax.dynamic_index_in_dim(halves, 1 - side, 0, False)
    keep = keep + swap(send, "tm", 1)
    hops = [("tm", 1 << bit) for bit in range(1, tm.bit_length() - 1)]
    hops += [("bus", 1 << bit) for bit in range(1, bus.bit_length() - 1)] + [("bus", 1)]
    for axis, distance in hops:
        sent = keep.astype(BF)
        keep = sent.astype(F32) + swap(sent, axis, distance).astype(F32)
    other = swap(keep, "tm", 1)
    return jnp.where(
        side == 0, jnp.concatenate([keep, other]), jnp.concatenate([other, keep])
    )


def shards(features, couplings, neighbors, w_graph, kernel_taps, w_out, cotangent):
    bus, tm = lax.axis_size("bus"), lax.axis_size("tm")
    rows, steps, chans = features.shape
    blocks, slots, half = couplings.shape[:3]
    up = [(i, i + 1) for i in range(bus - 1)]
    down = [(i + 1, i) for i in range(bus - 1)]
    wide = (steps, rows, chans)
    edge = (steps, half, chans)

    own, first, last, cot = call(
        split_body, [(wide, BF), (edge, BF), (edge, BF), (wide, BF)], features, cotangent
    )
    far = lax.ppermute(cot, "tm", [(2, 0), (3, 1)])
    before = lax.ppermute(last, "bus", up)
    after = lax.ppermute(first, "bus", down)
    near = lax.ppermute(cot, "tm", [(1, 0), (3, 2)])
    cross = lax.ppermute(far, "tm", [(1, 0), (0, 1)])

    position = neighbors - lax.axis_index("bus") * blocks + 1
    picks = (position[:, :, None] == jnp.arange(blocks + 2)[None, None]).astype(BF)
    mix = jnp.einsum("ikp,ikab->iapb", picks, couplings, preferred_element_type=F32)
    mix = mix.reshape(rows, (blocks + 2) * half).astype(BF)

    odd = lax.axis_index("tm") & 1
    slot = jnp.stack([jnp.where(odd == 0, 1, 3), jnp.where(odd == 0, 3, 1)]).astype(jnp.int32)
    pairs = 2 * steps + steps // 2
    grad_act, crossed = pl.pallas_call(
        conv_body,
        out_shape=[
            jax.ShapeDtypeStruct(wide, BF),
            jax.ShapeDtypeStruct((pairs, chans, 2 * rows), BF),
        ],
        in_specs=[pl.BlockSpec(memory_space=pltpu.SMEM)] + [VMEM] * 6,
        out_specs=[VMEM] * 2,
        scratch_shapes=[pltpu.VMEM((4,) + wide, BF), pltpu.VMEM((16 + 64, 8, chans), F32)],
        compiler_params=pltpu.CompilerParams(vmem_limit_bytes=LIMIT),
        cost_estimate=pl.CostEstimate(flops=1 << 31, bytes_accessed=1 << 20, transcendentals=0),
    )(slot, cot, near, far, cross, kernel_taps, w_out)

    act, spread, to_before, to_after, part_graph = call(
        main_body,
        [(wide, BF), (wide, F32), (edge, BF), (edge, BF), ((chans, chans), F32)],
        own, before, after, mix, mix.T, w_graph, grad_act,
    )
    from_after = lax.ppermute(to_before, "bus", down)
    from_before = lax.ppermute(to_after, "bus", up)

    taps8 = kernel_taps.astype(F32).reshape(-1, 4, chans)
    taps8 = jnp.concatenate([taps8, taps8], axis=1).reshape(-1, chans)
    part_out, part_lags = call(
        lag_body,
        [((chans, chans), F32), ((2 * tm * steps, chans), F32)],
        act, crossed, taps8, w_out,
        scratch=[
            pltpu.VMEM((steps // 2 + 1, 2 * rows, 2 * chans), BF),
            pltpu.VMEM((chans, chans), F32),
        ],
        flops=1 << 32,
    )
    part_lags = part_lags.reshape(-1, 2, 4, chans)[:, 0].reshape(-1, chans)
    summed = reduce_all(jnp.concatenate([part_graph, part_out, part_lags]), bus, tm)
    (grad_features,) = call(
        final_body, [(features.shape, BF)], spread, from_before, from_after, cotangent
    )
    scale = 1.0 / math.sqrt(bus * rows * steps * tm)
    summed = summed * scale
    return grad_features, summed[:chans], summed[chans : 2 * chans], summed[2 * chans :]


def solution(mesh):
    return jax.shard_map(
        shards,
        mesh=mesh,
        in_specs=(
            P("bus", "tm", None),
            P("bus", None, None, None),
            P("bus", None),
            P(),
            P(),
            P(),
            P("bus", "tm", None),
        ),
        out_specs=(P("bus", "tm", None), P(), P(), P()),
        check_vma=False,
    )
```

```python
import functools
import math

import jax
import jax.numpy as jnp
from jax import lax
from jax.experimental import pallas as pl
from jax.experimental.pallas import tpu as pltpu
from jax.sharding import PartitionSpec as P

BF = jnp.bfloat16
F32 = jnp.float32
VMEM = pl.BlockSpec(memory_space=pltpu.VMEM)
LIMIT = 16 << 20


def call(body, outs, *args, scratch=(), far=(), cost=1, kept=None):
    specs = [VMEM] * len(args)
    results = [VMEM] * len(outs)
    args = list(args)
    aliases = {}
    if kept is not None:
        results[kept[1]] = pl.BlockSpec(memory_space=pl.ANY)
        if kept[0] is not None:
            specs[kept[0]] = pl.BlockSpec(memory_space=pl.ANY)
            aliases = {kept[0]: kept[1]}
    for i in far:
        specs[i] = pl.BlockSpec(memory_space=pltpu.HBM)
        args[i] = pltpu.with_memory_space_constraint(args[i], pltpu.HBM)
    return pl.pallas_call(
        body,
        out_shape=[jax.ShapeDtypeStruct(shape, dtype) for shape, dtype in outs],
        in_specs=specs,
        out_specs=results,
        input_output_aliases=aliases,
        scratch_shapes=list(scratch),
        compiler_params=pltpu.CompilerParams(vmem_limit_bytes=LIMIT),
        cost_estimate=pl.CostEstimate(flops=cost, bytes_accessed=1, transcendentals=0),
    )(*args)


def dot(left, right, dims=((1,), (0,))):
    return lax.dot_general(left, right, (dims, ((), ())), preferred_element_type=F32)


def load_all(sems, pairs):
    copies = [
        pltpu.make_async_copy(source, target, sems.at[i])
        for i, (source, target) in enumerate(pairs)
    ]
    for copy in copies:
        copy.start()
    return copies


def split_body(source_ref, own_ref, near_ref, far_ref, feat_ref, sems):
    rows = feat_ref.shape[0]
    half = near_ref.shape[1]
    odd = lax.axis_index("bus") & 1
    for copy in load_all(sems, [(source_ref, feat_ref)]):
        copy.wait()
    for start in range(0, rows, 16):
        part = jnp.swapaxes(feat_ref[start : start + 16].astype(F32), 0, 1).astype(BF)
        own_ref[:, start : start + 16] = part
    low, high = pl.multiple_of(odd * half, half), pl.multiple_of((1 - odd) * half, half)
    near_ref[...] = own_ref[:, pl.ds(high, half)]
    far_ref[...] = own_ref[:, pl.ds(low, half)]


def take_block(block_ref, wout, steady, part, conv):
    steps, rows, chans = steady.shape
    for start in range(0, rows, 16):
        steady[:, start : start + 16] = jnp.swapaxes(
            block_ref[start : start + 16].astype(F32), 0, 1
        ).astype(BF)
    for s in range(0, steps, 4):
        block = steady[s : s + 4].reshape(4 * rows, chans)
        conv[s : s + 4] = dot(block, wout, ((1,), (1,))).astype(BF).reshape(4, rows, chans)
    for s in range(0, steps, 2):
        part[s // 2, :, 0:rows] = steady[s].T
        part[s // 2, :, rows : 2 * rows] = steady[s + 1].T


def place_part(part, cross_ref, slot, sem):
    size = part.shape[0]
    copy = pltpu.make_async_copy(part, cross_ref.at[pl.ds(slot * size, size)], sem)
    copy.start()
    return copy


def add_lags(sums, conv, lags_ref, base, where, causal):
    steps = conv.shape[0]
    for t in range(steps):
        value = conv[t, where, :].astype(F32)
        for s in range(steps):
            if causal and t < s:
                continue
            tap = lags_ref[base + (t - s)]
            sums[s][0] += tap * value[:8]
            sums[s][1] += tap * value[8:]


def early_body(
    ids_src, coup_src, cot_src, taps_src, wout_src, wg_src, near_ref,
    sum_ref, cross_ref, mix_ref, mixt_ref, steady_ref, taps_ref, wout_ref, wg_ref, lags_ref,
    part, conv, other, other_part, other_conv, dense, coup_ref, cot_ref, ids_ref, sems,
):
    copies = load_all(
        sems,
        [
            (cot_src, cot_ref), (wout_src, wout_ref), (taps_src, taps_ref),
            (coup_src, coup_ref), (wg_src, wg_ref), (ids_src, ids_ref),
        ],
    )
    for copy in copies:
        copy.wait()
    rows, steps, chans = cot_ref.shape
    blocks, slots, half = coup_ref.shape[:3]
    bus = lax.axis_index("bus")
    first = bus * blocks - 1
    turned = (bus & 1) == 0
    odd = lax.axis_index("tm") & 1
    take_block(cot_ref, wout_ref[...], steady_ref, part, conv)
    sent = [place_part(part, cross_ref, 0, sems.at[6])]
    take_block(near_ref, wout_ref[...], other, other_part, other_conv)
    sent.append(place_part(other_part, cross_ref, 1 + 2 * odd, sems.at[7]))
    taps = taps_ref[...].astype(F32)
    for lag in range(taps_ref.shape[0]):
        lags_ref[lag] = jnp.broadcast_to(taps[lag : lag + 1], (8, chans))

    def tile(index, carry):
        where = pl.ds(pl.multiple_of(index * 16, 16), 16)
        sums = [[jnp.zeros((8, chans), F32)] * 2 for _ in range(steps)]
        add_lags(sums, conv, lags_ref, 0, where, True)
        add_lags(sums, other_conv, lags_ref, steps, where, False)
        for s in range(steps):
            sum_ref[s, where, :] = jnp.concatenate(sums[s], axis=0)
        return carry

    lax.fori_loop(0, rows // 16, tile, 0)
    dense[...] = jnp.zeros_like(dense)
    for i in range(blocks):
        for k in range(slots):
            place = ids_ref[i, k] - first
            edge = (place == 0) | (place == blocks + 1)
            place = jnp.where(turned & edge, blocks + 1 - place, place)
            dense[i, place] += coup_ref[i, k].astype(F32)
    full = jnp.concatenate(
        [
            jnp.concatenate([dense[i, j] for j in range(blocks + 2)], axis=1)
            for i in range(blocks)
        ],
        axis=0,
    )
    mix_ref[...] = full.astype(BF)
    mixt_ref[...] = full.T.astype(BF)
    for copy in sent:
        copy.wait()


def add_body(last, sum_ref, crossed_ref, block_ref, lags_ref, wout_ref, out_ref, cross_ref, steady, part, conv, sems):
    steps, rows, chans = conv.shape
    slot = 3 - 2 * (lax.axis_index("tm") & 1) if last else 2
    take_block(block_ref, wout_ref[...], steady, part, conv)
    sent = place_part(part, cross_ref, slot, sems.at[0])

    def tile(index, carry):
        where = pl.ds(pl.multiple_of(index * 16, 16), 16)
        sums = [[sum_ref[s, where, :][:8], sum_ref[s, where, :][8:]] for s in range(steps)]
        add_lags(sums, conv, lags_ref, slot * steps, where, False)
        for s in range(steps):
            out_ref[s, where, :] = jnp.concatenate(sums[s], axis=0).astype(out_ref.dtype)
        return carry

    lax.fori_loop(0, rows // 16, tile, 0)
    sent.wait()


def forward_body(
    own_ref, before_ref, after_ref, mix_ref, wg_ref, act_ref, slope_ref, mixed_ref
):
    steps, rows, chans = own_ref.shape
    group = 4
    mix, wg = mix_ref[...], wg_ref[...]
    for s in range(0, steps, group):
        ext = jnp.concatenate(
            [
                jnp.concatenate([before_ref[t], own_ref[t], after_ref[t]], axis=0)
                for t in range(s, s + group)
            ],
            axis=1,
        )
        mixed = dot(mix, ext).astype(BF)
        mixed = jnp.concatenate(
            [mixed[:, t * chans : (t + 1) * chans] for t in range(group)], axis=0
        )
        mixed_ref[s : s + group] = mixed.reshape(group, rows, chans)
        pre = dot(mixed, wg)
        gate = 1.0 / (1.0 + jnp.exp(-pre))
        act_ref[s : s + group] = (pre * gate).astype(BF).reshape(group, rows, chans)
        slope = gate * (1.0 + pre * (1.0 - gate))
        slope_ref[s : s + group] = slope.reshape(group, rows, chans)


def backward_body(
    grad_ref, slope_ref, mixed_ref, mixt_ref, wg_ref, spread_ref, down_ref, up_ref, graph_ref
):
    steps, rows, chans = grad_ref.shape
    half = down_ref.shape[1]
    group = 4
    mixt, wg = mixt_ref[...], wg_ref[...]
    graph = jnp.zeros((chans, chans), F32)
    for s in range(0, steps, group):
        grad = grad_ref[s : s + group].astype(F32) * slope_ref[s : s + group]
        grad_pre = grad.astype(BF).reshape(group * rows, chans)
        mixed = mixed_ref[s : s + group].reshape(group * rows, chans)
        graph += dot(mixed, grad_pre, ((0,), (0,)))
        grad_mixed = dot(grad_pre, wg, ((1,), (1,))).astype(BF)
        grad_mixed = jnp.concatenate(
            [grad_mixed[t * rows : (t + 1) * rows] for t in range(group)], axis=1
        )
        spread = dot(mixt, grad_mixed)
        for t in range(group):
            part = spread[:, t * chans : (t + 1) * chans]
            down_ref[s + t] = part[:half].astype(BF)
            spread_ref[s + t] = part[half : half + rows]
            up_ref[s + t] = part[half + rows :].astype(BF)
    graph_ref[...] = graph


def lag_body(act_ref, cross_ref, taps_ref, wout_ref, graph_ref, keep_ref, send_ref, stack, pack):
    steps, rows, chans = act_ref.shape
    pairs = cross_ref.shape[0]
    group = steps // 2
    zero = jnp.zeros((rows, chans), BF)
    for i in range(group + 1):
        s = 2 * i
        if s < steps:
            stack[i, 0:rows, 0:chans] = act_ref[s]
            stack[i, rows : 2 * rows, 0:chans] = act_ref[s + 1]
            stack[i, rows : 2 * rows, chans : 2 * chans] = act_ref[s]
        else:
            stack[i, 0:rows, 0:chans] = zero
        stack[i, 0:rows, chans : 2 * chans] = act_ref[s - 1] if s > 0 else zero
    weight = wout_ref[...].astype(F32).T
    taps = taps_ref[...].astype(F32)
    out = jnp.zeros((chans, chans), F32)
    found = []
    for at in range(0, pairs, group):
        total = [None] * group
        for i in range(group + 1):
            count = min(group, pairs - at - i)
            if count <= 0:
                continue
            depth = 2 * rows if i < group else rows
            left = cross_ref[at + i : at + i + count, :, 0:depth].reshape(count * rows, depth)
            part = dot(left, stack[i, 0:depth])
            for g in range(count):
                piece = part[g * rows : (g + 1) * rows]
                total[g] = piece if total[g] is None else total[g] + piece
        for g in range(group):
            for side in range(2):
                lag = 2 * (at + g) + side
                part = total[g][:, side * chans : (side + 1) * chans]
                out += part * taps[lag : lag + 1]
                found.append(jnp.sum(part * weight, axis=0, keepdims=True))
    pack[0:chans] = graph_ref[...]
    pack[chans : 2 * chans] = out.T
    pack[2 * chans :] = jnp.concatenate(found, axis=0)
    odd = lax.axis_index("tm") & 1
    size = keep_ref.shape[0]
    keep_ref[...] = pack[pl.ds(pl.multiple_of(odd * size, size), size)]
    send_ref[...] = pack[pl.ds(pl.multiple_of((1 - odd) * size, size), size)]


def fold_body(low_bus, spread_ref, edge_ref, out_ref):
    half = edge_ref.shape[1]
    odd = lax.axis_index("bus") & 1
    at = pl.multiple_of((odd if low_bus else 1 - odd) * half, half)
    rest = pl.multiple_of((1 - odd if low_bus else odd) * half, half)
    for s in range(spread_ref.shape[0]):
        out_ref[s, pl.ds(rest, half)] = spread_ref[s, pl.ds(rest, half)]
        out_ref[s, pl.ds(at, half)] = spread_ref[s, pl.ds(at, half)] + edge_ref[s].astype(F32)


def final_body(spread_ref, even_ref, cot_ref, out_ref, sum_ref):
    rows = spread_ref.shape[1]
    half = even_ref.shape[1]
    odd = lax.axis_index("bus") & 1
    for start in range(0, rows, 16):
        sum_ref[:, start : start + 16] = spread_ref[:, start : start + 16] + cot_ref[
            :, start : start + 16
        ].astype(F32)
    at = pl.multiple_of((1 - odd) * half, half)
    sum_ref[:, pl.ds(at, half)] += even_ref[...].astype(F32)
    for start in range(0, rows, 16):
        out_ref[start : start + 16] = jnp.swapaxes(sum_ref[:, start : start + 16], 0, 1).astype(BF)


def pause_body(value_ref, last_ref, out_ref):
    out_ref[...] = value_ref[0:8] + last_ref[...]


def finish_body(scale, mine_ref, other_ref, mark_ref, graph_ref, out_ref, taps_ref, pack):
    odd = lax.axis_index("tm") & 1
    size = mine_ref.shape[0]
    chans = graph_ref.shape[0]
    pack[pl.ds(pl.multiple_of(odd * size, size), size)] = mine_ref[...] * scale
    pack[pl.ds(pl.multiple_of((1 - odd) * size, size), size)] = other_ref[...] * scale
    graph_ref[...] = pack[0:chans]
    out_ref[...] = pack[chans : 2 * chans]
    taps_ref[...] = pack[2 * chans :]


def swap(value, axis, distance):
    size = lax.axis_size(axis)
    return lax.ppermute(value, axis, [(i, i ^ distance) for i in range(size)])


def pause(value, received, mark):
    (mark,) = call(pause_body, [(mark.shape, F32)], value, mark, cost=1 << 36)
    return lax.optimization_barrier((received, mark))


def shards(features, couplings, neighbors, w_graph, kernel_taps, w_out, cotangent):
    bus, tm = lax.axis_size("bus"), lax.axis_size("tm")
    rows, steps, chans = features.shape
    blocks, slots, half = couplings.shape[:3]
    total = kernel_taps.shape[0]
    evens = [(i, i ^ 1) for i in range(bus)]
    odds = [(i, i + 1) for i in range(1, bus - 1, 2)] + [(i + 1, i) for i in range(1, bus - 1, 2)]
    wide = (steps, rows, chans)
    edge = (steps, half, chans)
    square = (chans, chans)

    own, even_edge, odd_edge = call(
        split_body, [(wide, BF), (edge, BF), (edge, BF)], features,
        scratch=[pltpu.VMEM(features.shape, BF), pltpu.SemaphoreType.DMA((1,))], far=[0],
    )
    near = lax.ppermute(cotangent, "tm", [(1, 0), (3, 2)])
    odd_edge = lax.ppermute(odd_edge, "bus", odds)
    even_edge = lax.ppermute(even_edge, "bus", evens)
    far = lax.ppermute(cotangent, "tm", [(2, 0), (3, 1)])

    pairs = total // 2
    crossing = (pairs, chans, 2 * rows)
    ext = rows + 2 * half
    part = pltpu.VMEM((steps // 2, chans, 2 * rows), BF)
    sums, crossed, mix, mixt, steady, taps, wout, wg, lags = call(
        early_body,
        [
            (wide, F32), (crossing, BF), ((rows, ext), BF), ((ext, rows), BF), (wide, BF),
            (kernel_taps.shape, BF), (square, BF), (square, BF), ((total, 8, chans), F32),
        ],
        neighbors, couplings, cotangent, kernel_taps, w_out, w_graph, near,
        scratch=[
            part, pltpu.VMEM(wide, BF), pltpu.VMEM(wide, BF), part, pltpu.VMEM(wide, BF),
            pltpu.VMEM((blocks, blocks + 2, half, half), F32),
            pltpu.VMEM(couplings.shape, BF),
            pltpu.VMEM(cotangent.shape, BF),
            pltpu.SMEM(neighbors.shape, jnp.int32),
            pltpu.SemaphoreType.DMA((8,)),
        ],
        far=range(6), kept=(None, 1),
    )

    def add_block(last, dtype, sums, crossed, block):
        return call(
            functools.partial(add_body, last), [(wide, dtype), (crossing, BF)],
            sums, crossed, block, lags, wout,
            scratch=[
                pltpu.VMEM(wide, BF), part, pltpu.VMEM(wide, BF), pltpu.SemaphoreType.DMA((1,))
            ],
            kept=(1, 1),
        )

    far, sums = lax.optimization_barrier((far, sums))
    swapped = lax.ppermute(far, "tm", [(1, 0), (0, 1)])
    sums, crossed = add_block(False, F32, sums, crossed, far)
    even_edge, odd_edge, sums = lax.optimization_barrier((even_edge, odd_edge, sums))
    act, slope, mixed = call(
        forward_body, [(wide, BF), (wide, F32), (wide, BF)], own, even_edge, odd_edge, mix, wg,
        cost=1 << 36,
    )
    swapped, act = lax.optimization_barrier((swapped, act))
    grad_act, crossed = add_block(True, BF, sums, crossed, swapped)
    spread, even_grad, odd_grad, part_graph = call(
        backward_body,
        [(wide, F32), (edge, BF), (edge, BF), (square, F32)],
        grad_act, slope, mixed, mixt, wg,
    )

    size = (2 * chans + total) // 2
    keep, send = call(
        lag_body, [((size, chans), F32), ((size, chans), F32)],
        act, crossed, taps, wout, part_graph,
        scratch=[
            pltpu.VMEM((steps // 2 + 1, 2 * rows, 2 * chans), BF),
            pltpu.VMEM((2 * size, chans), F32),
        ],
    )
    mark = send[0:8]
    keep = keep + swap(send, "tm", 1)
    hops = [("tm", 1 << bit) for bit in range(1, tm.bit_length() - 1)]
    hops += [("bus", 1 << bit) for bit in range(1, bus.bit_length() - 1)] + [("bus", 1)]
    odd_grad = lax.ppermute(odd_grad, "bus", odds)
    even_grad = lax.ppermute(even_grad, "bus", evens)
    for place, (axis, distance) in enumerate(hops):
        sent = keep.astype(BF)
        received = swap(sent, axis, distance)
        if place == 1:
            (spread,) = call(
                functools.partial(fold_body, True), [(wide, F32)], spread, odd_grad, cost=1 << 30
            )
            spread, mark = lax.optimization_barrier((spread, mark))
            received, mark = pause(keep, received, mark)
        if place == len(hops) - 2:
            (grad_features,) = call(
                final_body, [(features.shape, BF)], spread, even_grad, steady,
                scratch=[pltpu.VMEM(wide, F32)], cost=1 << 36,
            )
            received, grad_features = lax.optimization_barrier((received, grad_features))
        keep = sent.astype(F32) + received.astype(F32)
    other = swap(keep, "tm", 1)
    scale = 1.0 / math.sqrt(bus * rows * steps * tm)
    grad_graph, grad_out, grad_taps = call(
        functools.partial(finish_body, scale),
        [(square, F32), (square, F32), ((total, chans), F32)],
        keep, other, mark,
        scratch=[pltpu.VMEM((2 * size, chans), F32)],
    )
    return grad_features, grad_graph, grad_out, grad_taps


def solution(mesh):
    return jax.shard_map(
        shards,
        mesh=mesh,
        in_specs=(
            P("bus", "tm", None),
            P("bus", None, None, None),
            P("bus", None),
            P(),
            P(),
            P(),
            P("bus", "tm", None),
        ),
        out_specs=(P("bus", "tm", None), P(), P(), P()),
        check_vma=False,
    )
```

```python
import functools
import math

import jax
import jax.numpy as jnp
from jax import lax
from jax.experimental import pallas as pl
from jax.experimental.pallas import tpu as pltpu
from jax.sharding import PartitionSpec as P

BF = jnp.bfloat16
F32 = jnp.float32
VMEM = pl.BlockSpec(memory_space=pltpu.VMEM)
LIMIT = 16 << 20


def call(body, outs, *args, scratch=(), far=(), cost=1, kept=None):
    specs = [VMEM] * len(args)
    results = [VMEM] * len(outs)
    args = list(args)
    aliases = {}
    if kept is not None:
        results[kept[1]] = pl.BlockSpec(memory_space=pl.ANY)
        if kept[0] is not None:
            specs[kept[0]] = pl.BlockSpec(memory_space=pl.ANY)
            aliases = {kept[0]: kept[1]}
    for i in far:
        specs[i] = pl.BlockSpec(memory_space=pltpu.HBM)
        args[i] = pltpu.with_memory_space_constraint(args[i], pltpu.HBM)
    return pl.pallas_call(
        body,
        out_shape=[jax.ShapeDtypeStruct(shape, dtype) for shape, dtype in outs],
        in_specs=specs,
        out_specs=results,
        input_output_aliases=aliases,
        scratch_shapes=list(scratch),
        compiler_params=pltpu.CompilerParams(vmem_limit_bytes=LIMIT),
        cost_estimate=pl.CostEstimate(flops=cost, bytes_accessed=1, transcendentals=0),
    )(*args)


def dot(left, right, dims=((1,), (0,))):
    return lax.dot_general(left, right, (dims, ((), ())), preferred_element_type=F32)


def load_all(sems, pairs):
    copies = [
        pltpu.make_async_copy(source, target, sems.at[i])
        for i, (source, target) in enumerate(pairs)
    ]
    for copy in copies:
        copy.start()
    return copies


def split_body(source_ref, own_ref, near_ref, far_ref, feat_ref, sems):
    rows = feat_ref.shape[0]
    half = near_ref.shape[1]
    odd = lax.axis_index("bus") & 1
    for copy in load_all(sems, [(source_ref, feat_ref)]):
        copy.wait()
    for start in range(0, rows, 16):
        part = jnp.swapaxes(feat_ref[start : start + 16].astype(F32), 0, 1).astype(BF)
        own_ref[:, start : start + 16] = part
    low, high = pl.multiple_of(odd * half, half), pl.multiple_of((1 - odd) * half, half)
    near_ref[...] = own_ref[:, pl.ds(high, half)]
    far_ref[...] = own_ref[:, pl.ds(low, half)]


def take_block(block_ref, wout, steady, part, conv, valid=None):
    steps, rows, chans = steady.shape
    for start in range(0, rows, 16):
        block = block_ref[start : start + 16].astype(F32)
        if valid is not None:
            block = jnp.where(valid, block, 0.0)
        steady[:, start : start + 16] = jnp.swapaxes(block, 0, 1).astype(BF)
    for s in range(0, steps, 4):
        block = steady[s : s + 4].reshape(4 * rows, chans)
        conv[s : s + 4] = dot(block, wout, ((1,), (1,))).astype(BF).reshape(4, rows, chans)
    for s in range(0, steps, 2):
        part[s // 2, :, 0:rows] = steady[s].T
        part[s // 2, :, rows : 2 * rows] = steady[s + 1].T


def place_part(part, cross_ref, slot, sem):
    size = part.shape[0]
    copy = pltpu.make_async_copy(part, cross_ref.at[pl.ds(slot * size, size)], sem)
    copy.start()
    return copy


def add_lags(sums, conv, lags_ref, base, where, causal):
    steps = conv.shape[0]
    for t in range(steps):
        value = conv[t, where, :].astype(F32)
        for s in range(steps):
            if causal and t < s:
                continue
            tap = lags_ref[base + (t - s)]
            sums[s][0] += tap * value[:8]
            sums[s][1] += tap * value[8:]


def early_body(
    ids_src, coup_src, cot_src, taps_src, wout_src, wg_src, near_ref,
    sum_ref, cross_ref, mix_ref, mixt_ref, steady_ref, taps_ref, wout_ref, wg_ref, lags_ref,
    part, conv, other, other_part, other_conv, dense, coup_ref, cot_ref, ids_ref, sems,
):
    copies = load_all(
        sems,
        [
            (cot_src, cot_ref), (wout_src, wout_ref), (taps_src, taps_ref),
            (coup_src, coup_ref), (wg_src, wg_ref), (ids_src, ids_ref),
        ],
    )
    for copy in copies:
        copy.wait()
    rows, steps, chans = cot_ref.shape
    blocks, slots, half = coup_ref.shape[:3]
    bus = lax.axis_index("bus")
    first = bus * blocks - 1
    turned = (bus & 1) == 0
    odd = lax.axis_index("tm") & 1
    take_block(cot_ref, wout_ref[...], steady_ref, part, conv)
    sent = [place_part(part, cross_ref, 0, sems.at[6])]
    take_block(near_ref, wout_ref[...], other, other_part, other_conv, odd == 0)
    sent.append(place_part(other_part, cross_ref, 1 + 2 * odd, sems.at[7]))
    taps = taps_ref[...].astype(F32)
    for lag in range(taps_ref.shape[0]):
        lags_ref[lag] = jnp.broadcast_to(taps[lag : lag + 1], (8, chans))

    def tile(index, carry):
        where = pl.ds(pl.multiple_of(index * 16, 16), 16)
        sums = [[jnp.zeros((8, chans), F32)] * 2 for _ in range(steps)]
        add_lags(sums, conv, lags_ref, 0, where, True)
        add_lags(sums, other_conv, lags_ref, steps, where, False)
        for s in range(steps):
            sum_ref[s, where, :] = jnp.concatenate(sums[s], axis=0)
        return carry

    lax.fori_loop(0, rows // 16, tile, 0)
    dense[...] = jnp.zeros_like(dense)
    for i in range(blocks):
        for k in range(slots):
            place = ids_ref[i, k] - first
            edge = (place == 0) | (place == blocks + 1)
            place = jnp.where(turned & edge, blocks + 1 - place, place)
            dense[i, place] += coup_ref[i, k].astype(F32)
    full = jnp.concatenate(
        [
            jnp.concatenate([dense[i, j] for j in range(blocks + 2)], axis=1)
            for i in range(blocks)
        ],
        axis=0,
    )
    mix_ref[...] = full.astype(BF)
    mixt_ref[...] = full.T.astype(BF)
    for copy in sent:
        copy.wait()


def add_body(last, sum_ref, crossed_ref, block_ref, lags_ref, wout_ref, out_ref, cross_ref, steady, part, conv, sems):
    steps, rows, chans = conv.shape
    slot = 3 - 2 * (lax.axis_index("tm") & 1) if last else 2
    valid = lax.axis_index("tm") < 2
    take_block(block_ref, wout_ref[...], steady, part, conv, valid)
    sent = place_part(part, cross_ref, slot, sems.at[0])

    def tile(index, carry):
        where = pl.ds(pl.multiple_of(index * 16, 16), 16)
        sums = [[sum_ref[s, where, :][:8], sum_ref[s, where, :][8:]] for s in range(steps)]
        add_lags(sums, conv, lags_ref, slot * steps, where, False)
        for s in range(steps):
            out_ref[s, where, :] = jnp.concatenate(sums[s], axis=0).astype(out_ref.dtype)
        return carry

    lax.fori_loop(0, rows // 16, tile, 0)
    sent.wait()


def forward_body(
    own_ref, before_ref, after_ref, mix_ref, wg_ref, act_ref, slope_ref, mixed_ref
):
    steps, rows, chans = own_ref.shape
    group = 4
    mix, wg = mix_ref[...], wg_ref[...]
    for s in range(0, steps, group):
        ext = jnp.concatenate(
            [
                jnp.concatenate([before_ref[t], own_ref[t], after_ref[t]], axis=0)
                for t in range(s, s + group)
            ],
            axis=1,
        )
        mixed = dot(mix, ext).astype(BF)
        mixed = jnp.concatenate(
            [mixed[:, t * chans : (t + 1) * chans] for t in range(group)], axis=0
        )
        mixed_ref[s : s + group] = mixed.reshape(group, rows, chans)
        pre = dot(mixed, wg)
        gate = 1.0 / (1.0 + jnp.exp(-pre))
        act_ref[s : s + group] = (pre * gate).astype(BF).reshape(group, rows, chans)
        slope = gate * (1.0 + pre * (1.0 - gate))
        slope_ref[s : s + group] = slope.reshape(group, rows, chans)


def backward_body(
    grad_ref, slope_ref, mixed_ref, mixt_ref, wg_ref, spread_ref, down_ref, up_ref, graph_ref
):
    steps, rows, chans = grad_ref.shape
    half = down_ref.shape[1]
    group = 4
    mixt, wg = mixt_ref[...], wg_ref[...]
    graph = jnp.zeros((chans, chans), F32)
    for s in range(0, steps, group):
        grad = grad_ref[s : s + group].astype(F32) * slope_ref[s : s + group]
        grad_pre = grad.astype(BF).reshape(group * rows, chans)
        mixed = mixed_ref[s : s + group].reshape(group * rows, chans)
        graph += dot(mixed, grad_pre, ((0,), (0,)))
        grad_mixed = dot(grad_pre, wg, ((1,), (1,))).astype(BF)
        grad_mixed = jnp.concatenate(
            [grad_mixed[t * rows : (t + 1) * rows] for t in range(group)], axis=1
        )
        spread = dot(mixt, grad_mixed)
        for t in range(group):
            part = spread[:, t * chans : (t + 1) * chans]
            down_ref[s + t] = part[:half].astype(BF)
            spread_ref[s + t] = part[half : half + rows]
            up_ref[s + t] = part[half + rows :].astype(BF)
    graph_ref[...] = graph


def lag_body(act_ref, cross_ref, taps_ref, wout_ref, graph_ref, keep_ref, send_ref, stack, pack):
    steps, rows, chans = act_ref.shape
    pairs = cross_ref.shape[0]
    group = steps // 2
    zero = jnp.zeros((rows, chans), BF)
    for i in range(group + 1):
        s = 2 * i
        if s < steps:
            stack[i, 0:rows, 0:chans] = act_ref[s]
            stack[i, rows : 2 * rows, 0:chans] = act_ref[s + 1]
            stack[i, rows : 2 * rows, chans : 2 * chans] = act_ref[s]
        else:
            stack[i, 0:rows, 0:chans] = zero
        stack[i, 0:rows, chans : 2 * chans] = act_ref[s - 1] if s > 0 else zero
    weight = wout_ref[...].astype(F32).T
    taps = taps_ref[...].astype(F32)
    out = jnp.zeros((chans, chans), F32)
    found = []
    for at in range(0, pairs, group):
        total = [None] * group
        for i in range(group + 1):
            count = min(group, pairs - at - i)
            if count <= 0:
                continue
            depth = 2 * rows if i < group else rows
            left = cross_ref[at + i : at + i + count, :, 0:depth].reshape(count * rows, depth)
            part = dot(left, stack[i, 0:depth])
            for g in range(count):
                piece = part[g * rows : (g + 1) * rows]
                total[g] = piece if total[g] is None else total[g] + piece
        for g in range(group):
            for side in range(2):
                lag = 2 * (at + g) + side
                part = total[g][:, side * chans : (side + 1) * chans]
                out += part * taps[lag : lag + 1]
                found.append(jnp.sum(part * weight, axis=0, keepdims=True))
    pack[0:chans] = graph_ref[...]
    pack[chans : 2 * chans] = out.T
    pack[2 * chans :] = jnp.concatenate(found, axis=0)
    odd = lax.axis_index("tm") & 1
    size = keep_ref.shape[0]
    keep_ref[...] = pack[pl.ds(pl.multiple_of(odd * size, size), size)]
    send_ref[...] = pack[pl.ds(pl.multiple_of((1 - odd) * size, size), size)]


def fold_body(low_bus, spread_ref, edge_ref, out_ref):
    half = edge_ref.shape[1]
    odd = lax.axis_index("bus") & 1
    at = pl.multiple_of((odd if low_bus else 1 - odd) * half, half)
    rest = pl.multiple_of((1 - odd if low_bus else odd) * half, half)
    for s in range(spread_ref.shape[0]):
        out_ref[s, pl.ds(rest, half)] = spread_ref[s, pl.ds(rest, half)]
        out_ref[s, pl.ds(at, half)] = spread_ref[s, pl.ds(at, half)] + edge_ref[s].astype(F32)


def final_body(spread_ref, even_ref, cot_ref, out_ref, sum_ref):
    rows = spread_ref.shape[1]
    half = even_ref.shape[1]
    odd = lax.axis_index("bus") & 1
    for start in range(0, rows, 16):
        sum_ref[:, start : start + 16] = spread_ref[:, start : start + 16] + cot_ref[
            :, start : start + 16
        ].astype(F32)
    at = pl.multiple_of((1 - odd) * half, half)
    sum_ref[:, pl.ds(at, half)] += even_ref[...].astype(F32)
    for start in range(0, rows, 16):
        out_ref[start : start + 16] = jnp.swapaxes(sum_ref[:, start : start + 16], 0, 1).astype(BF)


def pause_body(value_ref, last_ref, out_ref):
    out_ref[...] = value_ref[0:8] + last_ref[...]


def finish_body(scale, mine_ref, other_ref, mark_ref, graph_ref, out_ref, taps_ref, pack):
    odd = lax.axis_index("tm") & 1
    size = mine_ref.shape[0]
    chans = graph_ref.shape[0]
    pack[pl.ds(pl.multiple_of(odd * size, size), size)] = mine_ref[...] * scale
    pack[pl.ds(pl.multiple_of((1 - odd) * size, size), size)] = other_ref[...] * scale
    graph_ref[...] = pack[0:chans]
    out_ref[...] = pack[chans : 2 * chans]
    taps_ref[...] = pack[2 * chans :]


def swap(value, axis, distance):
    size = lax.axis_size(axis)
    return lax.ppermute(value, axis, [(i, i ^ distance) for i in range(size)])


def pause(value, received, mark):
    (mark,) = call(pause_body, [(mark.shape, F32)], value, mark, cost=1 << 36)
    return lax.optimization_barrier((received, mark))


def shards(features, couplings, neighbors, w_graph, kernel_taps, w_out, cotangent):
    bus, tm = lax.axis_size("bus"), lax.axis_size("tm")
    rows, steps, chans = features.shape
    blocks, slots, half = couplings.shape[:3]
    total = kernel_taps.shape[0]
    evens = [(i, i ^ 1) for i in range(bus)]
    odds = [(i, i + 1) for i in range(1, bus - 1, 2)] + [(i + 1, i) for i in range(1, bus - 1, 2)]
    odds += [(0, 0), (bus - 1, bus - 1)]
    wide = (steps, rows, chans)
    edge = (steps, half, chans)
    square = (chans, chans)

    own, even_edge, odd_edge = call(
        split_body, [(wide, BF), (edge, BF), (edge, BF)], features,
        scratch=[pltpu.VMEM(features.shape, BF), pltpu.SemaphoreType.DMA((1,))], far=[0],
    )
    near = swap(cotangent, "tm", 1)
    odd_edge = lax.ppermute(odd_edge, "bus", odds)
    even_edge = lax.ppermute(even_edge, "bus", evens)
    far = swap(cotangent, "tm", 2)

    pairs = total // 2
    crossing = (pairs, chans, 2 * rows)
    ext = rows + 2 * half
    part = pltpu.VMEM((steps // 2, chans, 2 * rows), BF)
    sums, crossed, mix, mixt, steady, taps, wout, wg, lags = call(
        early_body,
        [
            (wide, F32), (crossing, BF), ((rows, ext), BF), ((ext, rows), BF), (wide, BF),
            (kernel_taps.shape, BF), (square, BF), (square, BF), ((total, 8, chans), F32),
        ],
        neighbors, couplings, cotangent, kernel_taps, w_out, w_graph, near,
        scratch=[
            part, pltpu.VMEM(wide, BF), pltpu.VMEM(wide, BF), part, pltpu.VMEM(wide, BF),
            pltpu.VMEM((blocks, blocks + 2, half, half), F32),
            pltpu.VMEM(couplings.shape, BF),
            pltpu.VMEM(cotangent.shape, BF),
            pltpu.SMEM(neighbors.shape, jnp.int32),
            pltpu.SemaphoreType.DMA((8,)),
        ],
        far=range(6), kept=(None, 1),
    )

    def add_block(last, dtype, sums, crossed, block):
        return call(
            functools.partial(add_body, last), [(wide, dtype), (crossing, BF)],
            sums, crossed, block, lags, wout,
            scratch=[
                pltpu.VMEM(wide, BF), part, pltpu.VMEM(wide, BF), pltpu.SemaphoreType.DMA((1,))
            ],
            kept=(1, 1),
        )

    far, sums = lax.optimization_barrier((far, sums))
    swapped = swap(far, "tm", 1)
    sums, crossed = add_block(False, F32, sums, crossed, far)
    even_edge, odd_edge, sums = lax.optimization_barrier((even_edge, odd_edge, sums))
    act, slope, mixed = call(
        forward_body, [(wide, BF), (wide, F32), (wide, BF)], own, even_edge, odd_edge, mix, wg,
        cost=1 << 36,
    )
    swapped, act = lax.optimization_barrier((swapped, act))
    grad_act, crossed = add_block(True, BF, sums, crossed, swapped)
    spread, even_grad, odd_grad, part_graph = call(
        backward_body,
        [(wide, F32), (edge, BF), (edge, BF), (square, F32)],
        grad_act, slope, mixed, mixt, wg,
    )

    size = (2 * chans + total) // 2
    keep, send = call(
        lag_body, [((size, chans), F32), ((size, chans), F32)],
        act, crossed, taps, wout, part_graph,
        scratch=[
            pltpu.VMEM((steps // 2 + 1, 2 * rows, 2 * chans), BF),
            pltpu.VMEM((2 * size, chans), F32),
        ],
    )
    mark = send[0:8]
    keep = keep + swap(send, "tm", 1)
    keep, even_grad = lax.optimization_barrier((keep, even_grad))
    hops = [("tm", 1 << bit) for bit in range(1, tm.bit_length() - 1)]
    hops += [("bus", 1 << bit) for bit in range(1, bus.bit_length() - 1)] + [("bus", 1)]
    odd_grad = lax.ppermute(odd_grad, "bus", odds)
    even_grad = lax.ppermute(even_grad, "bus", evens)
    for place, (axis, distance) in enumerate(hops):
        sent = keep.astype(BF)
        received = swap(sent, axis, distance)
        if place == 0:
            received, mark = pause(keep, received, mark)
        if place == 1:
            (spread,) = call(
                functools.partial(fold_body, True), [(wide, F32)], spread, odd_grad, cost=1 << 30
            )
            spread, mark = lax.optimization_barrier((spread, mark))
            received, mark = pause(keep, received, mark)
        if place == len(hops) - 2:
            (grad_features,) = call(
                final_body, [(features.shape, BF)], spread, even_grad, steady,
                scratch=[pltpu.VMEM(wide, F32)], cost=1 << 36,
            )
            received, grad_features = lax.optimization_barrier((received, grad_features))
        keep = sent.astype(F32) + received.astype(F32)
    other = swap(keep, "tm", 1)
    scale = 1.0 / math.sqrt(bus * rows * steps * tm)
    grad_graph, grad_out, grad_taps = call(
        functools.partial(finish_body, scale),
        [(square, F32), (square, F32), ((total, chans), F32)],
        keep, other, mark,
        scratch=[pltpu.VMEM((2 * size, chans), F32)],
    )
    return grad_features, grad_graph, grad_out, grad_taps


def solution(mesh):
    return jax.shard_map(
        shards,
        mesh=mesh,
        in_specs=(
            P("bus", "tm", None),
            P("bus", None, None, None),
            P("bus", None),
            P(),
            P(),
            P(),
            P("bus", "tm", None),
        ),
        out_specs=(P("bus", "tm", None), P(), P(), P()),
        check_vma=False,
    )
```

```python
import functools
import math

import jax
import jax.numpy as jnp
from jax import lax
from jax.experimental import pallas as pl
from jax.experimental.pallas import tpu as pltpu
from jax.sharding import PartitionSpec as P

BF = jnp.bfloat16
F32 = jnp.float32
VMEM = pl.BlockSpec(memory_space=pltpu.VMEM)
LIMIT = 16 << 20


def call(body, outs, *args, scratch=(), far=(), cost=1, kept=None, anywhere=()):
    specs = [VMEM] * len(args)
    results = [VMEM] * len(outs)
    args = list(args)
    for i in anywhere:
        specs[i] = pl.BlockSpec(memory_space=pl.ANY)
    aliases = {}
    if kept is not None:
        results[kept[1]] = pl.BlockSpec(memory_space=pl.ANY)
        if kept[0] is not None:
            specs[kept[0]] = pl.BlockSpec(memory_space=pl.ANY)
            aliases = {kept[0]: kept[1]}
    for i in far:
        specs[i] = pl.BlockSpec(memory_space=pltpu.HBM)
        args[i] = pltpu.with_memory_space_constraint(args[i], pltpu.HBM)
    return pl.pallas_call(
        body,
        out_shape=[jax.ShapeDtypeStruct(shape, dtype) for shape, dtype in outs],
        in_specs=specs,
        out_specs=results,
        input_output_aliases=aliases,
        scratch_shapes=list(scratch),
        compiler_params=pltpu.CompilerParams(vmem_limit_bytes=LIMIT),
        cost_estimate=pl.CostEstimate(flops=cost, bytes_accessed=1, transcendentals=0),
    )(*args)


def dot(left, right, dims=((1,), (0,))):
    return lax.dot_general(left, right, (dims, ((), ())), preferred_element_type=F32)


def load_all(sems, pairs):
    copies = [
        pltpu.make_async_copy(source, target, sems.at[i])
        for i, (source, target) in enumerate(pairs)
    ]
    for copy in copies:
        copy.start()
    return copies


def edge_body(even, source_ref, edge_ref, feat_ref, sems):
    half = feat_ref.shape[0]
    odd = lax.axis_index("bus") & 1
    first = pl.multiple_of((1 - odd if even else odd) * half, half)
    copies = load_all(
        sems,
        [
            (source_ref.at[pl.ds(first + start, 16)], feat_ref.at[pl.ds(start, 16)])
            for start in range(0, half, 16)
        ],
    )
    for copy, start in zip(copies, range(0, half, 16)):
        copy.wait()
        edge_ref[:, start : start + 16] = jnp.swapaxes(
            feat_ref[start : start + 16].astype(F32), 0, 1
        ).astype(BF)


def take_block(block_ref, wout, steady, part, conv, valid=None):
    steps, rows, chans = steady.shape
    for start in range(0, rows, 16):
        block = block_ref[start : start + 16].astype(F32)
        if valid is not None:
            block = jnp.where(valid, block, 0.0)
        steady[:, start : start + 16] = jnp.swapaxes(block, 0, 1).astype(BF)
    for s in range(0, steps, 4):
        block = steady[s : s + 4].reshape(4 * rows, chans)
        conv[s : s + 4] = dot(block, wout, ((1,), (1,))).astype(BF).reshape(4, rows, chans)
    for s in range(0, steps, 2):
        part[s // 2, :, 0:rows] = steady[s].T
        part[s // 2, :, rows : 2 * rows] = steady[s + 1].T


def place_part(part, cross_ref, slot, sem):
    size = part.shape[0]
    copy = pltpu.make_async_copy(part, cross_ref.at[pl.ds(slot * size, size)], sem)
    copy.start()
    return copy


def add_lags(sums, conv, lags_ref, base, where, causal):
    steps = conv.shape[0]
    for t in range(steps):
        value = conv[t, where, :].astype(F32)
        for s in range(steps):
            if causal and t < s:
                continue
            tap = lags_ref[base + (t - s)]
            sums[s][0] += tap * value[:8]
            sums[s][1] += tap * value[8:]


def early_body(
    ids_src, coup_src, cot_src, taps_src, wout_src, wg_src, near_ref,
    sum_ref, cross_ref, mix_ref, mixt_ref, steady_ref, taps_ref, wout_ref, wg_ref, lags_ref,
    part, conv, other, other_part, other_conv, dense, coup_ref, cot_ref, ids_ref, sems,
):
    copies = load_all(
        sems,
        [
            (cot_src, cot_ref), (wout_src, wout_ref), (taps_src, taps_ref),
            (coup_src, coup_ref), (wg_src, wg_ref), (ids_src, ids_ref),
        ],
    )
    for copy in copies:
        copy.wait()
    rows, steps, chans = cot_ref.shape
    blocks, slots, half = coup_ref.shape[:3]
    bus = lax.axis_index("bus")
    first = bus * blocks - 1
    turned = (bus & 1) == 0
    odd = lax.axis_index("tm") & 1
    take_block(cot_ref, wout_ref[...], steady_ref, part, conv)
    sent = [place_part(part, cross_ref, 0, sems.at[6])]
    take_block(near_ref, wout_ref[...], other, other_part, other_conv, odd == 0)
    sent.append(place_part(other_part, cross_ref, 1 + 2 * odd, sems.at[7]))
    taps = taps_ref[...].astype(F32)
    for lag in range(taps_ref.shape[0]):
        lags_ref[lag] = jnp.broadcast_to(taps[lag : lag + 1], (8, chans))

    def tile(index, carry):
        where = pl.ds(pl.multiple_of(index * 16, 16), 16)
        sums = [[jnp.zeros((8, chans), F32)] * 2 for _ in range(steps)]
        add_lags(sums, conv, lags_ref, 0, where, True)
        add_lags(sums, other_conv, lags_ref, steps, where, False)
        for s in range(steps):
            sum_ref[s, where, :] = jnp.concatenate(sums[s], axis=0)
        return carry

    lax.fori_loop(0, rows // 16, tile, 0)
    dense[...] = jnp.zeros_like(dense)
    for i in range(blocks):
        for k in range(slots):
            place = ids_ref[i, k] - first
            place = jnp.where(turned, blocks + 1 - place, place)
            dense[i, place] += coup_ref[i, k].astype(F32)
    full = jnp.concatenate(
        [
            jnp.concatenate([dense[i, j] for j in range(blocks + 2)], axis=1)
            for i in range(blocks)
        ],
        axis=0,
    )
    mix_ref[...] = full.astype(BF)
    mixt_ref[...] = full.T.astype(BF)
    for copy in sent:
        copy.wait()


def far_body(sum_ref, crossed_ref, block_ref, lags_ref, wout_ref, out_ref, cross_ref, steady, part, conv, sems):
    steps, rows, chans = conv.shape
    take_block(block_ref, wout_ref[...], steady, part, conv, lax.axis_index("tm") < 2)
    sent = place_part(part, cross_ref, 2, sems.at[0])

    def tile(index, carry):
        where = pl.ds(pl.multiple_of(index * 16, 16), 16)
        sums = [[sum_ref[s, where, :][:8], sum_ref[s, where, :][8:]] for s in range(steps)]
        add_lags(sums, conv, lags_ref, 2 * steps, where, False)
        for s in range(steps):
            out_ref[s, where, :] = jnp.concatenate(sums[s], axis=0)
        return carry

    lax.fori_loop(0, rows // 16, tile, 0)
    sent.wait()


def lag_steps(sum_ref, conv, lags, base, grad_ref, start):
    steps = grad_ref.shape[0]
    where = slice(start, start + 16)
    sums = []
    for s in range(steps):
        value = sum_ref[s, where, :]
        sums.append([value[:8], value[8:]])
    for t in range(steps):
        value = conv[t, where, :].astype(F32)
        for s in range(steps):
            tap = lags[base + (t - s)]
            sums[s][0] += tap * value[:8]
            sums[s][1] += tap * value[8:]
        yield
    for s in range(steps):
        grad_ref[s, where, :] = jnp.concatenate(sums[s], axis=0).astype(BF)
    yield


def tail_body(
    even_own, odd_own, even_ref, odd_ref, mix_ref, mixt_ref, wg_ref, wout_ref, taps_ref, lags_ref,
    sum_ref, swapped_ref, crossed_ref, mark_ref,
    keep_ref, send_ref, spread_ref, even_out, odd_out,
    slope_ref, mixed_ref, stack, steady, conv, cross, window, grad_ref, pack, sems,
):
    steps, rows, chans = mixed_ref.shape
    half = even_ref.shape[1]
    pairs = cross.shape[0]
    tm = lax.axis_index("tm")
    odd = tm & 1
    block = steps // 2
    near_at, slot = 1 + 2 * odd, 3 - 2 * odd
    copies = []
    for i, at in enumerate((0, near_at, 2)):
        where = pl.ds(at * block, block)
        copies.append(pltpu.make_async_copy(crossed_ref.at[where], cross.at[where], sems.at[i]))
        copies[-1].start()

    group = 4
    mix, wg = mix_ref[...], wg_ref[...]
    zero = jnp.zeros((rows, chans), BF)
    stack[0, 0:rows, chans : 2 * chans] = zero
    stack[block, 0:rows, 0:chans] = zero
    for s in range(0, steps, group):
        ext = jnp.concatenate(
            [
                jnp.concatenate([even_ref[t], even_own[t], odd_own[t], odd_ref[t]], axis=0)
                for t in range(s, s + group)
            ],
            axis=1,
        )
        mixed = dot(mix, ext).astype(BF)
        mixed = jnp.concatenate(
            [mixed[:, t * chans : (t + 1) * chans] for t in range(group)], axis=0
        )
        mixed_ref[s : s + group] = mixed.reshape(group, rows, chans)
        pre = dot(mixed, wg)
        gate = 1.0 / (1.0 + jnp.exp(-pre))
        act = (pre * gate).astype(BF).reshape(group, rows, chans)
        slope = gate * (1.0 + pre * (1.0 - gate))
        slope_ref[s : s + group] = slope.reshape(group, rows, chans)
        for t in range(s, s + group):
            low = (t % 2) * rows
            stack[t // 2, low : low + rows, 0:chans] = act[t - s]
            low = ((t + 1) % 2) * rows
            stack[(t + 1) // 2, low : low + rows, chans : 2 * chans] = act[t - s]

    take_block(swapped_ref, wout_ref[...], steady, cross.at[pl.ds(slot * block, block)], conv, tm < 2)
    window[0:31] = lags_ref[pl.ds(slot * steps - 15, 31)]
    for copy in copies:
        copy.wait()

    weight = wout_ref[...].astype(F32).T
    taps = taps_ref[...].astype(F32)
    out = jnp.zeros((chans, chans), F32)
    found = []
    for at in range(0, pairs, group):
        work = lag_steps(sum_ref, conv, window, 15, grad_ref, at * 4)
        total = [None] * group
        for i in range(block + 1):
            count = min(group, pairs - at - i)
            if count > 0:
                depth = 2 * rows if i < block else rows
                left = cross[at + i : at + i + count, :, 0:depth].reshape(count * rows, depth)
                part = dot(left, stack[i, 0:depth])
                for g in range(count):
                    piece = part[g * rows : (g + 1) * rows]
                    total[g] = piece if total[g] is None else total[g] + piece
            for _ in range(2):
                next(work, None)
        for _ in work:
            pass
        for g in range(group):
            for side in range(2):
                lag = 2 * (at + g) + side
                part = total[g][:, side * chans : (side + 1) * chans]
                out += part * taps[lag : lag + 1]
                found.append(jnp.sum(part * weight, axis=0, keepdims=True))

    mixt = mixt_ref[...]
    graph = jnp.zeros((chans, chans), F32)
    for s in range(0, steps, group):
        grad = grad_ref[s : s + group].astype(F32) * slope_ref[s : s + group]
        grad_pre = grad.astype(BF).reshape(group * rows, chans)
        mixed = mixed_ref[s : s + group].reshape(group * rows, chans)
        graph += dot(mixed, grad_pre, ((0,), (0,)))
        grad_mixed = dot(grad_pre, wg, ((1,), (1,))).astype(BF)
        grad_mixed = jnp.concatenate(
            [grad_mixed[t * rows : (t + 1) * rows] for t in range(group)], axis=1
        )
        spread = dot(mixt, grad_mixed)
        for t in range(group):
            part = spread[:, t * chans : (t + 1) * chans]
            even_out[s + t] = part[:half].astype(BF)
            spread_ref[s + t] = part[half : half + rows]
            odd_out[s + t] = part[half + rows :].astype(BF)

    pack[0:chans] = graph
    pack[chans : 2 * chans] = out.T
    pack[2 * chans :] = jnp.concatenate(found, axis=0)
    size = keep_ref.shape[0]
    keep_ref[...] = pack[pl.ds(pl.multiple_of(odd * size, size), size)]
    send_ref[...] = pack[pl.ds(pl.multiple_of((1 - odd) * size, size), size)]


def mark_body(first_ref, second_ref, mark_ref):
    mark_ref[...] = first_ref[0, 0:8].astype(F32) + second_ref[0, 0:8].astype(F32)


def fold_body(spread_ref, odd_edge_ref, cot_ref, out_ref):
    half = odd_edge_ref.shape[1]
    odd = lax.axis_index("bus") & 1
    low, high = pl.multiple_of(odd * half, half), pl.multiple_of((1 - odd) * half, half)
    for s in range(spread_ref.shape[0]):
        out_ref[s, :half] = spread_ref[s, :half] + cot_ref[s, pl.ds(high, half)].astype(F32)
        out_ref[s, half:] = (
            spread_ref[s, half:]
            + cot_ref[s, pl.ds(low, half)].astype(F32)
            + odd_edge_ref[s].astype(F32)
        )


def final_body(spread_ref, even_ref, out_ref):
    half = even_ref.shape[1]
    odd = lax.axis_index("bus") & 1
    for start in range(0, half, 16):
        part = spread_ref[:, start : start + 16] + even_ref[:, start : start + 16].astype(F32)
        where = pl.ds((1 - odd) * half + start, 16)
        out_ref[where] = jnp.swapaxes(part, 0, 1).astype(BF)
        part = spread_ref[:, half + start : half + start + 16]
        where = pl.ds(odd * half + start, 16)
        out_ref[where] = jnp.swapaxes(part, 0, 1).astype(BF)


def pause_body(value_ref, last_ref, out_ref):
    out_ref[...] = value_ref[0:8] + last_ref[...]


def finish_body(scale, mine_ref, other_ref, mark_ref, graph_ref, out_ref, taps_ref, pack):
    odd = lax.axis_index("tm") & 1
    size = mine_ref.shape[0]
    chans = graph_ref.shape[0]
    pack[pl.ds(pl.multiple_of(odd * size, size), size)] = mine_ref[...] * scale
    pack[pl.ds(pl.multiple_of((1 - odd) * size, size), size)] = other_ref[...] * scale
    graph_ref[...] = pack[0:chans]
    out_ref[...] = pack[chans : 2 * chans]
    taps_ref[...] = pack[2 * chans :]


def swap(value, axis, distance):
    size = lax.axis_size(axis)
    return lax.ppermute(value, axis, [(i, i ^ distance) for i in range(size)])


def pause(value, received, mark):
    (mark,) = call(pause_body, [(mark.shape, F32)], value, mark, cost=1 << 36)
    return lax.optimization_barrier((received, mark))


def shards(features, couplings, neighbors, w_graph, kernel_taps, w_out, cotangent):
    bus, tm = lax.axis_size("bus"), lax.axis_size("tm")
    rows, steps, chans = features.shape
    blocks, slots, half = couplings.shape[:3]
    total = kernel_taps.shape[0]
    evens = [(i, i ^ 1) for i in range(bus)]
    odds = [(i, i + 1) for i in range(1, bus - 1, 2)] + [(i + 1, i) for i in range(1, bus - 1, 2)]
    odds += [(0, 0), (bus - 1, bus - 1)]
    wide = (steps, rows, chans)
    edge = (steps, half, chans)
    square = (chans, chans)

    def edge_of(even):
        (found,) = call(
            functools.partial(edge_body, even), [(edge, BF)], features,
            scratch=[
                pltpu.VMEM((half,) + features.shape[1:], BF), pltpu.SemaphoreType.DMA((half // 16,))
            ],
            far=[0],
        )
        return found

    even_own, odd_own = edge_of(True), edge_of(False)
    near = swap(cotangent, "tm", 1)
    odd_edge = lax.ppermute(odd_own, "bus", odds)
    even_edge = lax.ppermute(even_own, "bus", evens)
    far = swap(cotangent, "tm", 2)

    pairs = total // 2
    crossing = (pairs, chans, 2 * rows)
    ext = rows + 2 * half
    part = pltpu.VMEM((steps // 2, chans, 2 * rows), BF)
    sums, crossed, mix, mixt, steady, taps, wout, wg, lags = call(
        early_body,
        [
            (wide, F32), (crossing, BF), ((rows, ext), BF), ((ext, rows), BF), (wide, BF),
            (kernel_taps.shape, BF), (square, BF), (square, BF), ((total, 8, chans), F32),
        ],
        neighbors, couplings, cotangent, kernel_taps, w_out, w_graph, near,
        scratch=[
            part, pltpu.VMEM(wide, BF), pltpu.VMEM(wide, BF), part, pltpu.VMEM(wide, BF),
            pltpu.VMEM((blocks, blocks + 2, half, half), F32),
            pltpu.VMEM(couplings.shape, BF),
            pltpu.VMEM(cotangent.shape, BF),
            pltpu.SMEM(neighbors.shape, jnp.int32),
            pltpu.SemaphoreType.DMA((8,)),
        ],
        far=range(6), kept=(None, 1),
    )

    far, sums = lax.optimization_barrier((far, sums))
    swapped = swap(far, "tm", 1)
    sums, crossed = call(
        far_body, [(wide, F32), (crossing, BF)], sums, crossed, far, lags, wout,
        scratch=[
            pltpu.VMEM(wide, BF), part, pltpu.VMEM(wide, BF), pltpu.SemaphoreType.DMA((1,))
        ],
        kept=(1, 1),
    )
    even_edge, odd_edge, sums = lax.optimization_barrier((even_edge, odd_edge, sums))
    (mark,) = call(mark_body, [((8, chans), F32)], even_edge, odd_edge, cost=1 << 36)
    swapped, mark = lax.optimization_barrier((swapped, mark))
    size = (2 * chans + total) // 2
    keep, send, spread, even_grad, odd_grad = call(
        tail_body,
        [((size, chans), F32), ((size, chans), F32), (wide, F32), (edge, BF), (edge, BF)],
        even_own, odd_own, even_edge, odd_edge, mix, mixt, wg, wout, taps, lags,
        sums, swapped, crossed, mark,
        scratch=[
            pltpu.VMEM(wide, F32), pltpu.VMEM(wide, BF),
            pltpu.VMEM((steps // 2 + 1, 2 * rows, 2 * chans), BF),
            pltpu.VMEM(wide, BF), pltpu.VMEM(wide, BF), pltpu.VMEM(crossing, BF),
            pltpu.VMEM((32, 8, chans), F32), pltpu.VMEM(wide, BF),
            pltpu.VMEM((2 * size, chans), F32), pltpu.SemaphoreType.DMA((3,)),
        ],
        anywhere=[12],
    )
    mark = send[0:8]
    keep = keep + swap(send, "tm", 1)
    hops = [("tm", 1 << bit) for bit in range(1, tm.bit_length() - 1)]
    hops += [("bus", 1 << bit) for bit in range(1, bus.bit_length() - 1)] + [("bus", 1)]
    odd_grad = lax.ppermute(odd_grad, "bus", odds)
    for place, (axis, distance) in enumerate(hops):
        sent = keep.astype(BF)
        received = swap(sent, axis, distance)
        if place < len(hops) - 2:
            received, mark = pause(keep, received, mark)
            if place == 0:
                even_grad, mark = lax.optimization_barrier((even_grad, mark))
                even_grad = lax.ppermute(even_grad, "bus", evens)
        elif place == len(hops) - 2:
            (spread,) = call(
                fold_body, [(wide, F32)], spread, odd_grad, steady, cost=1 << 36
            )
            received, spread = lax.optimization_barrier((received, spread))
        else:
            (grad_features,) = call(
                final_body, [(features.shape, BF)], spread, even_grad, cost=1 << 36
            )
            received, grad_features = lax.optimization_barrier((received, grad_features))
        keep = sent.astype(F32) + received.astype(F32)
    other = swap(keep, "tm", 1)
    scale = 1.0 / math.sqrt(bus * rows * steps * tm)
    grad_graph, grad_out, grad_taps = call(
        functools.partial(finish_body, scale),
        [(square, F32), (square, F32), ((total, chans), F32)],
        keep, other, mark,
        scratch=[pltpu.VMEM((2 * size, chans), F32)],
    )
    return grad_features, grad_graph, grad_out, grad_taps


def solution(mesh):
    return jax.shard_map(
        shards,
        mesh=mesh,
        in_specs=(
            P("bus", "tm", None),
            P("bus", None, None, None),
            P("bus", None),
            P(),
            P(),
            P(),
            P("bus", "tm", None),
        ),
        out_specs=(P("bus", "tm", None), P(), P(), P()),
        check_vma=False,
    )
```

```python
import functools
import itertools
import math

import jax
import jax.numpy as jnp
from jax import lax
from jax.experimental import pallas as pl
from jax.experimental.pallas import tpu as pltpu
from jax.sharding import PartitionSpec as P

BF = jnp.bfloat16
F32 = jnp.float32
VMEM = pl.BlockSpec(memory_space=pltpu.VMEM)
LIMIT = 16 << 20


def call(body, outs, *args, scratch=(), far=(), cost=1, kept=None, anywhere=()):
    specs = [VMEM] * len(args)
    results = [VMEM] * len(outs)
    args = list(args)
    for i in anywhere:
        specs[i] = pl.BlockSpec(memory_space=pl.ANY)
    aliases = {}
    if kept is not None:
        results[kept[1]] = pl.BlockSpec(memory_space=pl.ANY)
        if kept[0] is not None:
            specs[kept[0]] = pl.BlockSpec(memory_space=pl.ANY)
            aliases = {kept[0]: kept[1]}
    for i in far:
        specs[i] = pl.BlockSpec(memory_space=pltpu.HBM)
        args[i] = pltpu.with_memory_space_constraint(args[i], pltpu.HBM)
    return pl.pallas_call(
        body,
        out_shape=[jax.ShapeDtypeStruct(shape, dtype) for shape, dtype in outs],
        in_specs=specs,
        out_specs=results,
        input_output_aliases=aliases,
        scratch_shapes=list(scratch),
        compiler_params=pltpu.CompilerParams(vmem_limit_bytes=LIMIT),
        cost_estimate=pl.CostEstimate(flops=cost, bytes_accessed=1, transcendentals=0),
    )(*args)


def dot(left, right, dims=((1,), (0,))):
    return lax.dot_general(left, right, (dims, ((), ())), preferred_element_type=F32)


def load_all(sems, pairs):
    copies = [
        pltpu.make_async_copy(source, target, sems.at[i])
        for i, (source, target) in enumerate(pairs)
    ]
    for copy in copies:
        copy.start()
    return copies


def edge_body(even, source_ref, edge_ref, feat_ref, sems):
    half = feat_ref.shape[0]
    odd = lax.axis_index("bus") & 1
    first = pl.multiple_of((1 - odd if even else odd) * half, half)
    copies = load_all(
        sems,
        [
            (source_ref.at[pl.ds(first + start, 16)], feat_ref.at[pl.ds(start, 16)])
            for start in range(0, half, 16)
        ],
    )
    for copy, start in zip(copies, range(0, half, 16)):
        copy.wait()
        edge_ref[:, start : start + 16] = jnp.swapaxes(
            feat_ref[start : start + 16].astype(F32), 0, 1
        ).astype(BF)


def block_steps(block_ref, wout, steady, part, conv, valid=None):
    steps, rows, chans = steady.shape
    for start in range(0, rows, 16):
        block = block_ref[start : start + 16].astype(F32)
        if valid is not None:
            block = jnp.where(valid, block, 0.0)
        steady[:, start : start + 16] = jnp.swapaxes(block, 0, 1).astype(BF)
        yield
    for s in range(0, steps, 4):
        block = steady[s : s + 4].reshape(4 * rows, chans)
        conv[s : s + 4] = dot(block, wout, ((1,), (1,))).astype(BF).reshape(4, rows, chans)
        yield
    for s in range(0, steps, 2):
        part[s // 2, :, 0:rows] = steady[s].T
        part[s // 2, :, rows : 2 * rows] = steady[s + 1].T
        yield


def take_block(*args):
    for _ in block_steps(*args):
        pass


def place_part(part, cross_ref, slot, sem):
    size = part.shape[0]
    copy = pltpu.make_async_copy(part, cross_ref.at[pl.ds(slot * size, size)], sem)
    copy.start()
    return copy


def add_lags(sums, conv, lags_ref, base, where, causal):
    steps = conv.shape[0]
    for t in range(steps):
        value = conv[t, where, :].astype(F32)
        for s in range(steps):
            if causal and t < s:
                continue
            tap = lags_ref[base + (t - s)]
            sums[s][0] += tap * value[:8]
            sums[s][1] += tap * value[8:]


def early_body(
    ids_src, coup_src, cot_src, taps_src, wout_src, wg_src, near_ref,
    sum_ref, cross_ref, mix_ref, mixt_ref, steady_ref, taps_ref, wout_ref, wg_ref, lags_ref,
    part, conv, other, other_part, other_conv, dense, coup_ref, cot_ref, ids_ref, sems,
):
    copies = load_all(
        sems,
        [
            (cot_src, cot_ref), (wout_src, wout_ref), (taps_src, taps_ref),
            (coup_src, coup_ref), (wg_src, wg_ref), (ids_src, ids_ref),
        ],
    )
    for copy in copies:
        copy.wait()
    rows, steps, chans = cot_ref.shape
    blocks, slots, half = coup_ref.shape[:3]
    bus = lax.axis_index("bus")
    first = bus * blocks - 1
    turned = (bus & 1) == 0
    odd = lax.axis_index("tm") & 1
    take_block(cot_ref, wout_ref[...], steady_ref, part, conv)
    sent = [place_part(part, cross_ref, 0, sems.at[6])]
    take_block(near_ref, wout_ref[...], other, other_part, other_conv, odd == 0)
    sent.append(place_part(other_part, cross_ref, 1 + 2 * odd, sems.at[7]))
    taps = taps_ref[...].astype(F32)
    for lag in range(taps_ref.shape[0]):
        lags_ref[lag] = jnp.broadcast_to(taps[lag : lag + 1], (8, chans))

    def tile(index, carry):
        where = pl.ds(pl.multiple_of(index * 16, 16), 16)
        sums = [[jnp.zeros((8, chans), F32)] * 2 for _ in range(steps)]
        add_lags(sums, conv, lags_ref, 0, where, True)
        add_lags(sums, other_conv, lags_ref, steps, where, False)
        for s in range(steps):
            sum_ref[s, where, :] = jnp.concatenate(sums[s], axis=0)
        return carry

    lax.fori_loop(0, rows // 16, tile, 0)
    dense[...] = jnp.zeros_like(dense)
    for i in range(blocks):
        for k in range(slots):
            place = ids_ref[i, k] - first
            place = jnp.where(turned, blocks + 1 - place, place)
            dense[i, place] += coup_ref[i, k].astype(F32)
    full = jnp.concatenate(
        [
            jnp.concatenate([dense[i, j] for j in range(blocks + 2)], axis=1)
            for i in range(blocks)
        ],
        axis=0,
    )
    mix_ref[...] = full.astype(BF)
    mixt_ref[...] = full.T.astype(BF)
    for copy in sent:
        copy.wait()


def far_body(sum_ref, crossed_ref, block_ref, lags_ref, wout_ref, out_ref, cross_ref, steady, part, conv, sems):
    steps, rows, chans = conv.shape
    valid = lax.axis_index("tm") < 2

    @pl.when(valid)
    def _():
        take_block(block_ref, wout_ref[...], steady, part, conv)
        sent = place_part(part, cross_ref, 2, sems.at[0])

        def tile(index, carry):
            where = pl.ds(pl.multiple_of(index * 16, 16), 16)
            sums = [[sum_ref[s, where, :][:8], sum_ref[s, where, :][8:]] for s in range(steps)]
            add_lags(sums, conv, lags_ref, 2 * steps, where, False)
            for s in range(steps):
                out_ref[s, where, :] = jnp.concatenate(sums[s], axis=0)
            return carry

        lax.fori_loop(0, rows // 16, tile, 0)
        sent.wait()

    @pl.when(jnp.logical_not(valid))
    def _():
        part[...] = jnp.zeros_like(part)
        sent = place_part(part, cross_ref, 2, sems.at[0])
        out_ref[...] = sum_ref[...]
        sent.wait()


def lag_steps(sum_ref, conv, lags, base, grad_ref, start):
    steps = grad_ref.shape[0]
    where = slice(start, start + 16)
    sums = []
    for s in range(steps):
        value = sum_ref[s, where, :]
        sums.append([value[:8], value[8:]])
    for t in range(steps):
        value = conv[t, where, :].astype(F32)
        for s in range(steps):
            tap = lags[base + (t - s)]
            sums[s][0] += tap * value[:8]
            sums[s][1] += tap * value[8:]
        yield
    for s in range(steps):
        grad_ref[s, where, :] = jnp.concatenate(sums[s], axis=0).astype(BF)
    yield


def tail_body(
    even_own, odd_own, even_ref, odd_ref, mix_ref, mixt_ref, wg_ref, wout_ref, taps_ref, lags_ref,
    sum_ref, swapped_ref, crossed_ref, mark_ref,
    keep_ref, send_ref, spread_ref, even_out, odd_out,
    slope_ref, mixed_ref, stack, steady, conv, cross, window, grad_ref, pack, sems,
):
    steps, rows, chans = mixed_ref.shape
    half = even_ref.shape[1]
    pairs = cross.shape[0]
    tm = lax.axis_index("tm")
    odd = tm & 1
    block = steps // 2
    near_at, slot = 1 + 2 * odd, 3 - 2 * odd
    copies = []
    for i, at in enumerate((0, near_at, 2)):
        where = pl.ds(at * block, block)
        copies.append(pltpu.make_async_copy(crossed_ref.at[where], cross.at[where], sems.at[i]))
        copies[-1].start()

    group = 4
    mix, wg = mix_ref[...], wg_ref[...]
    zero = jnp.zeros((rows, chans), BF)
    other = block_steps(
        swapped_ref, wout_ref[...], steady, cross.at[pl.ds(slot * block, block)], conv, tm < 2
    )
    stack[0, 0:rows, chans : 2 * chans] = zero
    stack[block, 0:rows, 0:chans] = zero
    for s in range(0, steps, group):
        ext = jnp.concatenate(
            [
                jnp.concatenate([even_ref[t], even_own[t], odd_own[t], odd_ref[t]], axis=0)
                for t in range(s, s + group)
            ],
            axis=1,
        )
        mixed = dot(mix, ext).astype(BF)
        mixed = jnp.concatenate(
            [mixed[:, t * chans : (t + 1) * chans] for t in range(group)], axis=0
        )
        mixed_ref[s : s + group] = mixed.reshape(group, rows, chans)
        for _ in range(2):
            next(other, None)
        pre = dot(mixed, wg)
        gate = 0.5 + 0.5 * jnp.tanh(0.5 * pre)
        act = (pre * gate).astype(BF).reshape(group, rows, chans)
        slope = gate * (1.0 + pre * (1.0 - gate))
        slope_ref[s : s + group] = slope.reshape(group, rows, chans)
        for t in range(s, s + group):
            low = (t % 2) * rows
            stack[t // 2, low : low + rows, 0:chans] = act[t - s]
            low = ((t + 1) % 2) * rows
            stack[(t + 1) // 2, low : low + rows, chans : 2 * chans] = act[t - s]
        for _ in range(3):
            next(other, None)

    for _ in other:
        pass
    window[0:31] = lags_ref[pl.ds(slot * steps - 15, 31)]
    for copy in copies:
        copy.wait()

    weight = wout_ref[...].astype(F32).T
    taps = taps_ref[...].astype(F32)
    out_at, lag_at = chans, 2 * chans

    def lag_group(at, tiles):
        work = itertools.chain.from_iterable(
            [lag_steps(sum_ref, conv, window, 15, grad_ref, tile) for tile in tiles]
        )
        total = [None] * group
        for i in range(block + 1):
            count = min(group, pairs - at - i)
            if count > 0:
                depth = 2 * rows if i < block else rows
                left = cross[at + i : at + i + count, :, 0:depth].reshape(count * rows, depth)
                part = dot(left, stack[i, 0:depth])
                for g in range(count):
                    piece = part[g * rows : (g + 1) * rows]
                    total[g] = piece if total[g] is None else total[g] + piece
            for _ in range(4):
                next(work, None)
        for _ in work:
            pass
        out, found = jnp.zeros((chans, chans), F32), []
        for g in range(group):
            for side in range(2):
                lag = 2 * (at + g) + side
                part = total[g][:, side * chans : (side + 1) * chans]
                out += part * taps[lag : lag + 1]
                found.append(jnp.sum(part * weight, axis=0, keepdims=True))
        pack[lag_at + 2 * at : lag_at + 2 * (at + group)] = jnp.concatenate(found, axis=0)
        return out

    middle = pairs // 2
    out = jnp.zeros((chans, chans), F32)
    for at in range(0, middle, group):
        out += lag_group(at, range(at * 8, at * 8 + 32, 16))
    pack[out_at:lag_at] = out

    @pl.when(tm < 2)
    def _():
        out = pack[out_at:lag_at]
        for at in range(middle, pairs, group):
            out += lag_group(at, ())
        pack[out_at:lag_at] = out

    @pl.when(tm >= 2)
    def _():
        pack[lag_at + 2 * middle :] = jnp.zeros((2 * (pairs - middle), chans), F32)

    mixt = mixt_ref[...]
    graph = jnp.zeros((chans, chans), F32)
    for s in range(0, steps, group):
        grad = grad_ref[s : s + group].astype(F32) * slope_ref[s : s + group]
        grad_pre = grad.astype(BF).reshape(group * rows, chans)
        mixed = mixed_ref[s : s + group].reshape(group * rows, chans)
        graph += dot(mixed, grad_pre, ((0,), (0,)))
        grad_mixed = dot(grad_pre, wg, ((1,), (1,))).astype(BF)
        grad_mixed = jnp.concatenate(
            [grad_mixed[t * rows : (t + 1) * rows] for t in range(group)], axis=1
        )
        spread = dot(mixt, grad_mixed)
        for t in range(group):
            part = spread[:, t * chans : (t + 1) * chans]
            even_out[s + t] = part[:half].astype(BF)
            spread_ref[s + t] = part[half : half + rows]
            odd_out[s + t] = part[half + rows :].astype(BF)

    pack[0:chans] = graph
    pack[out_at:lag_at] = pack[out_at:lag_at].T
    size = keep_ref.shape[0]
    keep_ref[...] = pack[pl.ds(pl.multiple_of(odd * size, size), size)]
    send_ref[...] = pack[pl.ds(pl.multiple_of((1 - odd) * size, size), size)]


def mark_body(first_ref, second_ref, mark_ref):
    mark_ref[...] = first_ref[0, 0:8].astype(F32) + second_ref[0, 0:8].astype(F32)


def fold_body(spread_ref, cot_ref, out_ref):
    half = spread_ref.shape[1] // 2
    odd = lax.axis_index("bus") & 1
    low, high = pl.multiple_of(odd * half, half), pl.multiple_of((1 - odd) * half, half)
    for s in range(spread_ref.shape[0]):
        out_ref[s, :half] = spread_ref[s, :half] + cot_ref[s, pl.ds(high, half)].astype(F32)
        out_ref[s, half:] = spread_ref[s, half:] + cot_ref[s, pl.ds(low, half)].astype(F32)


def edge_add_body(spread_ref, even_ref, out_ref):
    half = even_ref.shape[1]
    for s in range(spread_ref.shape[0]):
        out_ref[s, :half] = spread_ref[s, :half] + even_ref[s].astype(F32)
        out_ref[s, half:] = spread_ref[s, half:]


def final_body(spread_ref, odd_ref, out_ref):
    half = odd_ref.shape[1]
    odd = lax.axis_index("bus") & 1
    for start in range(0, half, 16):
        part = spread_ref[:, start : start + 16]
        where = pl.ds((1 - odd) * half + start, 16)
        out_ref[where] = jnp.swapaxes(part, 0, 1).astype(BF)
        part = spread_ref[:, half + start : half + start + 16]
        part = part + odd_ref[:, start : start + 16].astype(F32)
        where = pl.ds(odd * half + start, 16)
        out_ref[where] = jnp.swapaxes(part, 0, 1).astype(BF)


def pause_body(value_ref, last_ref, out_ref):
    out_ref[...] = value_ref[0:8] + last_ref[...]


def finish_body(scale, mine_ref, other_ref, mark_ref, graph_ref, out_ref, taps_ref, pack):
    odd = lax.axis_index("tm") & 1
    size = mine_ref.shape[0]
    chans = graph_ref.shape[0]
    pack[pl.ds(pl.multiple_of(odd * size, size), size)] = mine_ref[...] * scale
    pack[pl.ds(pl.multiple_of((1 - odd) * size, size), size)] = other_ref[...] * scale
    graph_ref[...] = pack[0:chans]
    out_ref[...] = pack[chans : 2 * chans]
    taps_ref[...] = pack[2 * chans :]


def swap(value, axis, distance):
    size = lax.axis_size(axis)
    return lax.ppermute(value, axis, [(i, i ^ distance) for i in range(size)])


def pause(value, received, mark):
    (mark,) = call(pause_body, [(mark.shape, F32)], value, mark, cost=1 << 36)
    return lax.optimization_barrier((received, mark))


def shards(features, couplings, neighbors, w_graph, kernel_taps, w_out, cotangent):
    bus, tm = lax.axis_size("bus"), lax.axis_size("tm")
    rows, steps, chans = features.shape
    blocks, slots, half = couplings.shape[:3]
    total = kernel_taps.shape[0]
    evens = [(i, i ^ 1) for i in range(bus)]
    odds = [(i, i + 1) for i in range(1, bus - 1, 2)] + [(i + 1, i) for i in range(1, bus - 1, 2)]
    odds += [(0, 0), (bus - 1, bus - 1)]
    wide = (steps, rows, chans)
    edge = (steps, half, chans)
    square = (chans, chans)

    def edge_of(even):
        (found,) = call(
            functools.partial(edge_body, even), [(edge, BF)], features,
            scratch=[
                pltpu.VMEM((half,) + features.shape[1:], BF), pltpu.SemaphoreType.DMA((half // 16,))
            ],
            far=[0],
        )
        return found

    even_own, odd_own = edge_of(True), edge_of(False)
    near = swap(cotangent, "tm", 1)
    odd_edge = lax.ppermute(odd_own, "bus", odds)
    even_edge = lax.ppermute(even_own, "bus", evens)
    far = swap(cotangent, "tm", 2)

    pairs = total // 2
    crossing = (pairs, chans, 2 * rows)
    ext = rows + 2 * half
    part = pltpu.VMEM((steps // 2, chans, 2 * rows), BF)
    sums, crossed, mix, mixt, steady, taps, wout, wg, lags = call(
        early_body,
        [
            (wide, F32), (crossing, BF), ((rows, ext), BF), ((ext, rows), BF), (wide, BF),
            (kernel_taps.shape, BF), (square, BF), (square, BF), ((total, 8, chans), F32),
        ],
        neighbors, couplings, cotangent, kernel_taps, w_out, w_graph, near,
        scratch=[
            part, pltpu.VMEM(wide, BF), pltpu.VMEM(wide, BF), part, pltpu.VMEM(wide, BF),
            pltpu.VMEM((blocks, blocks + 2, half, half), F32),
            pltpu.VMEM(couplings.shape, BF),
            pltpu.VMEM(cotangent.shape, BF),
            pltpu.SMEM(neighbors.shape, jnp.int32),
            pltpu.SemaphoreType.DMA((8,)),
        ],
        far=range(6), kept=(None, 1),
    )

    far, sums = lax.optimization_barrier((far, sums))
    swapped = swap(far, "tm", 1)
    sums, crossed = call(
        far_body, [(wide, F32), (crossing, BF)], sums, crossed, far, lags, wout,
        scratch=[
            pltpu.VMEM(wide, BF), part, pltpu.VMEM(wide, BF), pltpu.SemaphoreType.DMA((1,))
        ],
        kept=(1, 1),
    )
    even_edge, odd_edge, sums = lax.optimization_barrier((even_edge, odd_edge, sums))
    (mark,) = call(mark_body, [((8, chans), F32)], even_edge, odd_edge, cost=1 << 36)
    swapped, mark = lax.optimization_barrier((swapped, mark))
    size = (2 * chans + total) // 2
    keep, send, spread, even_grad, odd_grad = call(
        tail_body,
        [((size, chans), F32), ((size, chans), F32), (wide, F32), (edge, BF), (edge, BF)],
        even_own, odd_own, even_edge, odd_edge, mix, mixt, wg, wout, taps, lags,
        sums, swapped, crossed, mark,
        scratch=[
            pltpu.VMEM(wide, F32), pltpu.VMEM(wide, BF),
            pltpu.VMEM((steps // 2 + 1, 2 * rows, 2 * chans), BF),
            pltpu.VMEM(wide, BF), pltpu.VMEM(wide, BF), pltpu.VMEM(crossing, BF),
            pltpu.VMEM((32, 8, chans), F32), pltpu.VMEM(wide, BF),
            pltpu.VMEM((2 * size, chans), F32), pltpu.SemaphoreType.DMA((3,)),
        ],
        anywhere=[12],
    )
    mark = send[0:8]
    odd_grad = lax.ppermute(odd_grad, "bus", evens)
    keep = keep + swap(send, "tm", 1)
    keep, even_grad = lax.optimization_barrier((keep, even_grad))
    even_grad = lax.ppermute(even_grad, "bus", evens)
    hops = [("bus", 1 << bit) for bit in range(1, bus.bit_length() - 1)]
    hops += [("tm", 1 << bit) for bit in range(1, tm.bit_length() - 1)] + [("bus", 1)]
    onward = [(i, i + 2) for i in range(0, bus - 2, 2)] + [(i, i - 2) for i in range(3, bus, 2)]
    for place, (axis, distance) in enumerate(hops):
        sent = keep.astype(BF)
        received = swap(sent, axis, distance)
        if place < len(hops) - 2:
            received, mark = pause(keep, received, mark)
            if place == 0:
                odd_grad, mark = lax.optimization_barrier((odd_grad, mark))
                odd_grad = lax.ppermute(odd_grad, "bus", onward)
        elif place == len(hops) - 2:
            (spread,) = call(fold_body, [(wide, F32)], spread, steady, cost=1 << 36)
            received, spread = lax.optimization_barrier((received, spread))
        else:
            (spread,) = call(edge_add_body, [(wide, F32)], spread, even_grad, cost=1 << 36)
            received, spread = lax.optimization_barrier((received, spread))
        keep = sent.astype(F32) + received.astype(F32)
    other = swap(keep, "tm", 1)
    (grad_features,) = call(
        final_body, [(features.shape, BF)], spread, odd_grad, cost=1 << 36
    )
    other, grad_features = lax.optimization_barrier((other, grad_features))
    scale = 1.0 / math.sqrt(bus * rows * steps * tm)
    grad_graph, grad_out, grad_taps = call(
        functools.partial(finish_body, scale),
        [(square, F32), (square, F32), ((total, chans), F32)],
        keep, other, mark,
        scratch=[pltpu.VMEM((2 * size, chans), F32)],
    )
    return grad_features, grad_graph, grad_out, grad_taps


def solution(mesh):
    return jax.shard_map(
        shards,
        mesh=mesh,
        in_specs=(
            P("bus", "tm", None),
            P("bus", None, None, None),
            P("bus", None),
            P(),
            P(),
            P(),
            P("bus", "tm", None),
        ),
        out_specs=(P("bus", "tm", None), P(), P(), P()),
        check_vma=False,
    )
```

```python
import functools
import itertools
import math

import jax
import jax.numpy as jnp
from jax import lax
from jax.experimental import pallas as pl
from jax.experimental.pallas import tpu as pltpu
from jax.sharding import PartitionSpec as P

BF = jnp.bfloat16
F32 = jnp.float32
VMEM = pl.BlockSpec(memory_space=pltpu.VMEM)
LIMIT = 16 << 20


def call(body, outs, *args, scratch=(), far=(), cost=1, kept=None, anywhere=()):
    specs = [VMEM] * len(args)
    results = [VMEM] * len(outs)
    args = list(args)
    for i in anywhere:
        specs[i] = pl.BlockSpec(memory_space=pl.ANY)
    aliases = {}
    if kept is not None:
        results[kept[1]] = pl.BlockSpec(memory_space=pl.ANY)
        if kept[0] is not None:
            specs[kept[0]] = pl.BlockSpec(memory_space=pl.ANY)
            aliases = {kept[0]: kept[1]}
    for i in far:
        specs[i] = pl.BlockSpec(memory_space=pltpu.HBM)
        args[i] = pltpu.with_memory_space_constraint(args[i], pltpu.HBM)
    return pl.pallas_call(
        body,
        out_shape=[jax.ShapeDtypeStruct(shape, dtype) for shape, dtype in outs],
        in_specs=specs,
        out_specs=results,
        input_output_aliases=aliases,
        scratch_shapes=list(scratch),
        compiler_params=pltpu.CompilerParams(vmem_limit_bytes=LIMIT),
        cost_estimate=pl.CostEstimate(flops=cost, bytes_accessed=1, transcendentals=0),
    )(*args)


def dot(left, right, dims=((1,), (0,))):
    return lax.dot_general(left, right, (dims, ((), ())), preferred_element_type=F32)


def doubled(weight):
    zero = jnp.zeros_like(weight)
    top = jnp.concatenate([weight, zero], axis=1)
    return jnp.concatenate([top, jnp.concatenate([zero, weight], axis=1)], axis=0)


def two_halves(values, weight, dims=((1,), (0,))):
    count, rows, chans = values.shape
    flat = values.reshape(count * rows, chans)
    middle = count * rows // 2
    both = dot(jnp.concatenate([flat[:middle], flat[middle:]], axis=1), weight, dims)
    return [
        both[t * rows : (t + 1) * rows, h * chans : (h + 1) * chans]
        for h in range(2)
        for t in range(count // 2)
    ]


def load_all(sems, pairs):
    copies = [
        pltpu.make_async_copy(source, target, sems.at[i])
        for i, (source, target) in enumerate(pairs)
    ]
    for copy in copies:
        copy.start()
    return copies


def edge_body(even, source_ref, edge_ref, feat_ref, sems):
    half = feat_ref.shape[0]
    odd = lax.axis_index("bus") & 1
    first = pl.multiple_of((1 - odd if even else odd) * half, half)
    copies = load_all(
        sems,
        [
            (source_ref.at[pl.ds(first + start, 16)], feat_ref.at[pl.ds(start, 16)])
            for start in range(0, half, 16)
        ],
    )
    for copy, start in zip(copies, range(0, half, 16)):
        copy.wait()
        edge_ref[:, start : start + 16] = jnp.swapaxes(
            feat_ref[start : start + 16].astype(F32), 0, 1
        ).astype(BF)


def block_steps(block_ref, wout, steady, part, conv, valid=None):
    steps, rows, chans = steady.shape
    for start in range(0, rows, 16):
        block = block_ref[start : start + 16].astype(F32)
        if valid is not None:
            block = jnp.where(valid, block, 0.0)
        steady[:, start : start + 16] = jnp.swapaxes(block, 0, 1).astype(BF)
        yield
    wout = doubled(wout)
    for s in range(0, steps, 8):
        for t, piece in enumerate(two_halves(steady[s : s + 8], wout, ((1,), (1,)))):
            conv[s + t] = piece.astype(BF)
        yield
    for s in range(0, steps, 2):
        part[s // 2, :, 0:rows] = steady[s].T
        part[s // 2, :, rows : 2 * rows] = steady[s + 1].T
        yield


def take_block(*args):
    for _ in block_steps(*args):
        pass


def place_part(part, cross_ref, slot, sem):
    size = part.shape[0]
    copy = pltpu.make_async_copy(part, cross_ref.at[pl.ds(slot * size, size)], sem)
    copy.start()
    return copy


def add_lags(sums, conv, lags_ref, base, where, causal):
    steps = conv.shape[0]
    for t in range(steps):
        value = conv[t, where, :].astype(F32)
        for s in range(steps):
            if causal and t < s:
                continue
            tap = lags_ref[base + (t - s)]
            sums[s][0] += tap * value[:8]
            sums[s][1] += tap * value[8:]


def early_body(
    ids_src, coup_src, cot_src, taps_src, wout_src, wg_src, near_ref,
    sum_ref, cross_ref, mix_ref, mixt_ref, steady_ref, taps_ref, wout_ref, wg_ref, lags_ref,
    part, conv, other, other_part, other_conv, dense, coup_ref, cot_ref, ids_ref, sems,
):
    copies = load_all(
        sems,
        [
            (cot_src, cot_ref), (wout_src, wout_ref), (taps_src, taps_ref),
            (coup_src, coup_ref), (wg_src, wg_ref), (ids_src, ids_ref),
        ],
    )
    for copy in copies:
        copy.wait()
    rows, steps, chans = cot_ref.shape
    blocks, slots, half = coup_ref.shape[:3]
    bus = lax.axis_index("bus")
    first = bus * blocks - 1
    turned = (bus & 1) == 0
    odd = lax.axis_index("tm") & 1
    take_block(cot_ref, wout_ref[...], steady_ref, part, conv)
    sent = [place_part(part, cross_ref, 0, sems.at[6])]
    take_block(near_ref, wout_ref[...], other, other_part, other_conv, odd == 0)
    sent.append(place_part(other_part, cross_ref, 1 + 2 * odd, sems.at[7]))
    taps = taps_ref[...].astype(F32)
    for lag in range(taps_ref.shape[0]):
        lags_ref[lag] = jnp.broadcast_to(taps[lag : lag + 1], (8, chans))

    def tile(index, carry):
        where = pl.ds(pl.multiple_of(index * 16, 16), 16)
        sums = [[jnp.zeros((8, chans), F32)] * 2 for _ in range(steps)]
        add_lags(sums, conv, lags_ref, 0, where, True)
        add_lags(sums, other_conv, lags_ref, steps, where, False)
        for s in range(steps):
            sum_ref[s, where, :] = jnp.concatenate(sums[s], axis=0)
        return carry

    lax.fori_loop(0, rows // 16, tile, 0)
    dense[...] = jnp.zeros_like(dense)
    for i in range(blocks):
        for k in range(slots):
            place = ids_ref[i, k] - first
            place = jnp.where(turned, blocks + 1 - place, place)
            dense[i, place] += coup_ref[i, k].astype(F32)
    full = jnp.concatenate(
        [
            jnp.concatenate([dense[i, j] for j in range(blocks + 2)], axis=1)
            for i in range(blocks)
        ],
        axis=0,
    )
    mix_ref[...] = full.astype(BF)
    mixt_ref[...] = full.T.astype(BF)
    for copy in sent:
        copy.wait()


def far_body(sum_ref, crossed_ref, block_ref, lags_ref, wout_ref, out_ref, cross_ref, steady, part, conv, sems):
    steps, rows, chans = conv.shape
    valid = lax.axis_index("tm") < 2

    @pl.when(valid)
    def _():
        take_block(block_ref, wout_ref[...], steady, part, conv)
        sent = place_part(part, cross_ref, 2, sems.at[0])

        def tile(index, carry):
            where = pl.ds(pl.multiple_of(index * 16, 16), 16)
            sums = [[sum_ref[s, where, :][:8], sum_ref[s, where, :][8:]] for s in range(steps)]
            add_lags(sums, conv, lags_ref, 2 * steps, where, False)
            for s in range(steps):
                out_ref[s, where, :] = jnp.concatenate(sums[s], axis=0)
            return carry

        lax.fori_loop(0, rows // 16, tile, 0)
        sent.wait()

    @pl.when(jnp.logical_not(valid))
    def _():
        part[...] = jnp.zeros_like(part)
        sent = place_part(part, cross_ref, 2, sems.at[0])
        out_ref[...] = sum_ref[...]
        sent.wait()


def lag_steps(sum_ref, conv, lags, base, grad_ref, start):
    steps = grad_ref.shape[0]
    where = slice(start, start + 16)
    sums = []
    for s in range(steps):
        value = sum_ref[s, where, :]
        sums.append([value[:8], value[8:]])
    for t in range(steps):
        value = conv[t, where, :].astype(F32)
        for s in range(steps):
            tap = lags[base + (t - s)]
            sums[s][0] += tap * value[:8]
            sums[s][1] += tap * value[8:]
        yield
    for s in range(steps):
        grad_ref[s, where, :] = jnp.concatenate(sums[s], axis=0).astype(BF)
    yield


def tail_body(
    even_own, odd_own, even_ref, odd_ref, mix_ref, mixt_ref, wg_ref, wout_ref, taps_ref, lags_ref,
    sum_ref, swapped_ref, crossed_ref, mark_ref,
    keep_ref, send_ref, spread_ref, even_out, odd_out,
    slope_ref, mixed_ref, stack, steady, conv, cross, window, grad_ref, pack, sems,
):
    steps, rows, chans = mixed_ref.shape
    half = even_ref.shape[1]
    pairs = cross.shape[0]
    tm = lax.axis_index("tm")
    odd = tm & 1
    block = steps // 2
    near_at, slot = 1 + 2 * odd, 3 - 2 * odd
    copies = []
    for i, at in enumerate((0, near_at, 2)):
        where = pl.ds(at * block, block)
        copies.append(pltpu.make_async_copy(crossed_ref.at[where], cross.at[where], sems.at[i]))
        copies[-1].start()

    group = 4
    mix, wg = mix_ref[...], doubled(wg_ref[...])
    zero = jnp.zeros((rows, chans), BF)
    other = block_steps(
        swapped_ref, wout_ref[...], steady, cross.at[pl.ds(slot * block, block)], conv, tm < 2
    )
    stack[0, 0:rows, chans : 2 * chans] = zero
    stack[block, 0:rows, chans : 2 * chans] = zero
    stack[block, rows : 2 * rows, 0:chans] = zero
    wide_group = 2 * group
    for s in range(0, steps, wide_group):
        mixed = []
        for start in range(s, s + wide_group, group):
            ext = jnp.concatenate(
                [
                    jnp.concatenate([even_ref[t], even_own[t], odd_own[t], odd_ref[t]], axis=0)
                    for t in range(start, start + group)
                ],
                axis=1,
            )
            found = dot(mix, ext).astype(BF)
            mixed += [found[:, t * chans : (t + 1) * chans] for t in range(group)]
            next(other, None)
        mixed = jnp.stack(mixed)
        mixed_ref[s : s + wide_group] = mixed
        for t, pre in enumerate(two_halves(mixed, wg), s):
            gate = 0.5 + 0.5 * jnp.tanh(0.5 * pre)
            act = (pre * gate).astype(BF)
            slope_ref[t] = gate * (1.0 + pre * (1.0 - gate))
            low = (t % 2) * rows
            stack[t // 2, low : low + rows, 0:chans] = act
            low = ((t + 1) % 2) * rows if t < steps - 1 else rows
            stack[(t + 1) // 2, low : low + rows, chans : 2 * chans] = act
            if t == steps - 1:
                stack[block, 0:rows, 0:chans] = act
            next(other, None)
    for _ in other:
        pass
    window[0:31] = lags_ref[pl.ds(slot * steps - 15, 31)]
    for copy in copies:
        copy.wait()

    weight = wout_ref[...].astype(F32).T
    taps = taps_ref[...].astype(F32)
    out_at, lag_at = chans, 2 * chans

    def lag_group(at, tiles):
        work = itertools.chain.from_iterable(
            [lag_steps(sum_ref, conv, window, 15, grad_ref, tile) for tile in tiles]
        )
        totals = []
        for first in (at, at + group):
            total = [None] * group
            for i in range(block):
                count = min(group, pairs - first - i)
                if count > 0:
                    left = cross[first + i : first + i + count].reshape(count * rows, 2 * rows)
                    part = dot(left, stack[i])
                    for g in range(count):
                        piece = part[g * rows : (g + 1) * rows]
                        total[g] = piece if total[g] is None else total[g] + piece
                for _ in range(5):
                    next(work, None)
            totals.append(total)
        for _ in work:
            pass
        last = None
        if at + 2 * group + block <= pairs:
            left = jnp.concatenate(
                [
                    cross[first + block : first + block + group, :, 0:rows].reshape(
                        group * rows, rows
                    )
                    for first in (at, at + group)
                ],
                axis=1,
            )
            last = dot(left, stack[block])
        out, found = jnp.zeros((chans, chans), F32), []
        for half_at, total in enumerate(totals):
            for g in range(group):
                for side in range(2):
                    lag = 2 * (at + half_at * group + g) + side
                    part = total[g][:, side * chans : (side + 1) * chans]
                    if side == 1 and last is not None:
                        lanes = slice(half_at * chans, (half_at + 1) * chans)
                        part = part + last[g * rows : (g + 1) * rows, lanes]
                    out += part * taps[lag : lag + 1]
                    found.append(jnp.sum(part * weight, axis=0, keepdims=True))
        pack[lag_at + 2 * at : lag_at + 2 * (at + 2 * group)] = jnp.concatenate(found, axis=0)
        return out

    middle = pairs // 2
    out = jnp.zeros((chans, chans), F32)
    for at in range(0, middle, 2 * group):
        out += lag_group(at, range(at * 8, at * 8 + 64, 16))
    pack[out_at:lag_at] = out

    @pl.when(tm < 2)
    def _():
        out = pack[out_at:lag_at]
        for at in range(middle, pairs, 2 * group):
            out += lag_group(at, ())
        pack[out_at:lag_at] = out

    @pl.when(tm >= 2)
    def _():
        pack[lag_at + 2 * middle :] = jnp.zeros((2 * (pairs - middle), chans), F32)

    mixt = mixt_ref[...]
    graph = jnp.zeros((chans, chans), F32)
    for s in range(0, steps, wide_group):
        grad = grad_ref[s : s + wide_group].astype(F32) * slope_ref[s : s + wide_group]
        grad_pre = grad.astype(BF)
        flat = (wide_group * rows, chans)
        mixed = mixed_ref[s : s + wide_group].reshape(flat)
        graph += dot(mixed, grad_pre.reshape(flat), ((0,), (0,)))
        grad_mixed = [piece.astype(BF) for piece in two_halves(grad_pre, wg, ((1,), (1,)))]
        for start in range(0, wide_group, group):
            spread = dot(mixt, jnp.concatenate(grad_mixed[start : start + group], axis=1))
            for t in range(group):
                part = spread[:, t * chans : (t + 1) * chans]
                even_out[s + start + t] = part[:half].astype(BF)
                spread_ref[s + start + t] = part[half : half + rows]
                odd_out[s + start + t] = part[half + rows :].astype(BF)

    pack[0:chans] = graph
    pack[out_at:lag_at] = pack[out_at:lag_at].T
    size = keep_ref.shape[0]
    keep_ref[...] = pack[pl.ds(pl.multiple_of(odd * size, size), size)]
    send_ref[...] = pack[pl.ds(pl.multiple_of((1 - odd) * size, size), size)]


def mark_body(first_ref, second_ref, mark_ref):
    mark_ref[...] = first_ref[0, 0:8].astype(F32) + second_ref[0, 0:8].astype(F32)


def fold_body(spread_ref, cot_ref, out_ref):
    half = spread_ref.shape[1] // 2
    odd = lax.axis_index("bus") & 1
    low, high = pl.multiple_of(odd * half, half), pl.multiple_of((1 - odd) * half, half)
    for s in range(spread_ref.shape[0]):
        out_ref[s, :half] = spread_ref[s, :half] + cot_ref[s, pl.ds(high, half)].astype(F32)
        out_ref[s, half:] = spread_ref[s, half:] + cot_ref[s, pl.ds(low, half)].astype(F32)


def edge_add_body(spread_ref, even_ref, out_ref):
    half = even_ref.shape[1]
    for s in range(spread_ref.shape[0]):
        out_ref[s, :half] = spread_ref[s, :half] + even_ref[s].astype(F32)
        out_ref[s, half:] = spread_ref[s, half:]


def final_body(spread_ref, odd_ref, out_ref):
    half = odd_ref.shape[1]
    odd = lax.axis_index("bus") & 1
    for start in range(0, half, 16):
        part = spread_ref[:, start : start + 16]
        where = pl.ds((1 - odd) * half + start, 16)
        out_ref[where] = jnp.swapaxes(part, 0, 1).astype(BF)
        part = spread_ref[:, half + start : half + start + 16]
        part = part + odd_ref[:, start : start + 16].astype(F32)
        where = pl.ds(odd * half + start, 16)
        out_ref[where] = jnp.swapaxes(part, 0, 1).astype(BF)


def pause_body(value_ref, last_ref, out_ref):
    out_ref[...] = value_ref[0:8] + last_ref[...]


def finish_body(scale, mine_ref, other_ref, mark_ref, graph_ref, out_ref, taps_ref, pack):
    odd = lax.axis_index("tm") & 1
    size = mine_ref.shape[0]
    chans = graph_ref.shape[0]
    pack[pl.ds(pl.multiple_of(odd * size, size), size)] = mine_ref[...] * scale
    pack[pl.ds(pl.multiple_of((1 - odd) * size, size), size)] = other_ref[...] * scale
    graph_ref[...] = pack[0:chans]
    out_ref[...] = pack[chans : 2 * chans]
    taps_ref[...] = pack[2 * chans :]


def swap(value, axis, distance):
    size = lax.axis_size(axis)
    return lax.ppermute(value, axis, [(i, i ^ distance) for i in range(size)])


def pause(value, received, mark):
    (mark,) = call(pause_body, [(mark.shape, F32)], value, mark, cost=1 << 36)
    return lax.optimization_barrier((received, mark))


def shards(features, couplings, neighbors, w_graph, kernel_taps, w_out, cotangent):
    bus, tm = lax.axis_size("bus"), lax.axis_size("tm")
    rows, steps, chans = features.shape
    blocks, slots, half = couplings.shape[:3]
    total = kernel_taps.shape[0]
    evens = [(i, i ^ 1) for i in range(bus)]
    odds = [(i, i + 1) for i in range(1, bus - 1, 2)] + [(i + 1, i) for i in range(1, bus - 1, 2)]
    odds += [(0, 0), (bus - 1, bus - 1)]
    wide = (steps, rows, chans)
    edge = (steps, half, chans)
    square = (chans, chans)

    def edge_of(even):
        (found,) = call(
            functools.partial(edge_body, even), [(edge, BF)], features,
            scratch=[
                pltpu.VMEM((half,) + features.shape[1:], BF), pltpu.SemaphoreType.DMA((half // 16,))
            ],
            far=[0],
        )
        return found

    even_own, odd_own = edge_of(True), edge_of(False)
    near = swap(cotangent, "tm", 1)
    odd_edge = lax.ppermute(odd_own, "bus", odds)
    even_edge = lax.ppermute(even_own, "bus", evens)
    far = swap(cotangent, "tm", 2)

    pairs = total // 2
    crossing = (pairs, chans, 2 * rows)
    ext = rows + 2 * half
    part = pltpu.VMEM((steps // 2, chans, 2 * rows), BF)
    sums, crossed, mix, mixt, steady, taps, wout, wg, lags = call(
        early_body,
        [
            (wide, F32), (crossing, BF), ((rows, ext), BF), ((ext, rows), BF), (wide, BF),
            (kernel_taps.shape, BF), (square, BF), (square, BF), ((total, 8, chans), F32),
        ],
        neighbors, couplings, cotangent, kernel_taps, w_out, w_graph, near,
        scratch=[
            part, pltpu.VMEM(wide, BF), pltpu.VMEM(wide, BF), part, pltpu.VMEM(wide, BF),
            pltpu.VMEM((blocks, blocks + 2, half, half), F32),
            pltpu.VMEM(couplings.shape, BF),
            pltpu.VMEM(cotangent.shape, BF),
            pltpu.SMEM(neighbors.shape, jnp.int32),
            pltpu.SemaphoreType.DMA((8,)),
        ],
        far=range(6), kept=(None, 1),
    )

    far, sums = lax.optimization_barrier((far, sums))
    swapped = swap(far, "tm", 1)
    sums, crossed = call(
        far_body, [(wide, F32), (crossing, BF)], sums, crossed, far, lags, wout,
        scratch=[
            pltpu.VMEM(wide, BF), part, pltpu.VMEM(wide, BF), pltpu.SemaphoreType.DMA((1,))
        ],
        kept=(1, 1),
    )
    even_edge, odd_edge, sums = lax.optimization_barrier((even_edge, odd_edge, sums))
    (mark,) = call(mark_body, [((8, chans), F32)], even_edge, odd_edge, cost=1 << 36)
    swapped, mark = lax.optimization_barrier((swapped, mark))
    size = (2 * chans + total) // 2
    keep, send, spread, even_grad, odd_grad = call(
        tail_body,
        [((size, chans), F32), ((size, chans), F32), (wide, F32), (edge, BF), (edge, BF)],
        even_own, odd_own, even_edge, odd_edge, mix, mixt, wg, wout, taps, lags,
        sums, swapped, crossed, mark,
        scratch=[
            pltpu.VMEM(wide, F32), pltpu.VMEM(wide, BF),
            pltpu.VMEM((steps // 2 + 1, 2 * rows, 2 * chans), BF),
            pltpu.VMEM(wide, BF), pltpu.VMEM(wide, BF), pltpu.VMEM(crossing, BF),
            pltpu.VMEM((32, 8, chans), F32), pltpu.VMEM(wide, BF),
            pltpu.VMEM((2 * size, chans), F32), pltpu.SemaphoreType.DMA((3,)),
        ],
        anywhere=[12],
    )
    mark = send[0:8]
    odd_grad = lax.ppermute(odd_grad, "bus", evens)
    keep = keep + swap(send, "tm", 1)
    keep, even_grad = lax.optimization_barrier((keep, even_grad))
    even_grad = lax.ppermute(even_grad, "bus", evens)
    hops = [("bus", 1 << bit) for bit in range(1, bus.bit_length() - 1)]
    hops += [("tm", 1 << bit) for bit in range(1, tm.bit_length() - 1)] + [("bus", 1)]
    onward = [(i, i + 2) for i in range(0, bus - 2, 2)] + [(i, i - 2) for i in range(3, bus, 2)]
    for place, (axis, distance) in enumerate(hops):
        sent = keep.astype(BF)
        received = swap(sent, axis, distance)
        if place < len(hops) - 2:
            received, mark = pause(keep, received, mark)
            if place == 0:
                odd_grad, mark = lax.optimization_barrier((odd_grad, mark))
                odd_grad = lax.ppermute(odd_grad, "bus", onward)
        elif place == len(hops) - 2:
            (spread,) = call(fold_body, [(wide, F32)], spread, steady, cost=1 << 36)
            received, spread = lax.optimization_barrier((received, spread))
        else:
            (spread,) = call(edge_add_body, [(wide, F32)], spread, even_grad, cost=1 << 36)
            received, spread = lax.optimization_barrier((received, spread))
        keep = sent.astype(F32) + received.astype(F32)
    other = swap(keep, "tm", 1)
    (grad_features,) = call(
        final_body, [(features.shape, BF)], spread, odd_grad, cost=1 << 36
    )
    other, grad_features = lax.optimization_barrier((other, grad_features))
    scale = 1.0 / math.sqrt(bus * rows * steps * tm)
    grad_graph, grad_out, grad_taps = call(
        functools.partial(finish_body, scale),
        [(square, F32), (square, F32), ((total, chans), F32)],
        keep, other, mark,
        scratch=[pltpu.VMEM((2 * size, chans), F32)],
    )
    return grad_features, grad_graph, grad_out, grad_taps


def solution(mesh):
    return jax.shard_map(
        shards,
        mesh=mesh,
        in_specs=(
            P("bus", "tm", None),
            P("bus", None, None, None),
            P("bus", None),
            P(),
            P(),
            P(),
            P("bus", "tm", None),
        ),
        out_specs=(P("bus", "tm", None), P(), P(), P()),
        check_vma=False,
    )
```

```python
import functools
import itertools
import math

import jax
import jax.numpy as jnp
from jax import lax
from jax.experimental import pallas as pl
from jax.experimental.pallas import tpu as pltpu
from jax.sharding import PartitionSpec as P

BF = jnp.bfloat16
F32 = jnp.float32
VMEM = pl.BlockSpec(memory_space=pltpu.VMEM)
LIMIT = 16 << 20


def call(body, outs, *args, scratch=(), far=(), cost=1, kept=None, anywhere=()):
    specs = [VMEM] * len(args)
    results = [VMEM] * len(outs)
    args = list(args)
    for i in anywhere:
        specs[i] = pl.BlockSpec(memory_space=pl.ANY)
    aliases = {}
    if kept is not None:
        results[kept[1]] = pl.BlockSpec(memory_space=pl.ANY)
        if kept[0] is not None:
            specs[kept[0]] = pl.BlockSpec(memory_space=pl.ANY)
            aliases = {kept[0]: kept[1]}
    for i in far:
        specs[i] = pl.BlockSpec(memory_space=pltpu.HBM)
        args[i] = pltpu.with_memory_space_constraint(args[i], pltpu.HBM)
    return pl.pallas_call(
        body,
        out_shape=[jax.ShapeDtypeStruct(shape, dtype) for shape, dtype in outs],
        in_specs=specs,
        out_specs=results,
        input_output_aliases=aliases,
        scratch_shapes=list(scratch),
        compiler_params=pltpu.CompilerParams(vmem_limit_bytes=LIMIT),
        cost_estimate=pl.CostEstimate(flops=cost, bytes_accessed=1, transcendentals=0),
    )(*args)


def dot(left, right, dims=((1,), (0,))):
    return lax.dot_general(left, right, (dims, ((), ())), preferred_element_type=F32)


def doubled(weight):
    zero = jnp.zeros_like(weight)
    top = jnp.concatenate([weight, zero], axis=1)
    return jnp.concatenate([top, jnp.concatenate([zero, weight], axis=1)], axis=0)


def two_halves(values, weight, dims=((1,), (0,))):
    count, rows, chans = values.shape
    flat = values.reshape(count * rows, chans)
    middle = count * rows // 2
    both = dot(jnp.concatenate([flat[:middle], flat[middle:]], axis=1), weight, dims)
    return [
        both[t * rows : (t + 1) * rows, h * chans : (h + 1) * chans]
        for h in range(2)
        for t in range(count // 2)
    ]


def load_all(sems, pairs):
    copies = [
        pltpu.make_async_copy(source, target, sems.at[i])
        for i, (source, target) in enumerate(pairs)
    ]
    for copy in copies:
        copy.start()
    return copies


def edge_body(even, source_ref, edge_ref, feat_ref, sems):
    half = feat_ref.shape[0]
    odd = lax.axis_index("bus") & 1
    first = pl.multiple_of((1 - odd if even else odd) * half, half)
    copies = load_all(
        sems,
        [
            (source_ref.at[pl.ds(first + start, 16)], feat_ref.at[pl.ds(start, 16)])
            for start in range(0, half, 16)
        ],
    )
    for copy, start in zip(copies, range(0, half, 16)):
        copy.wait()
        edge_ref[:, start : start + 16] = jnp.swapaxes(
            feat_ref[start : start + 16].astype(F32), 0, 1
        ).astype(BF)


def block_steps(block_ref, wout, steady, part, conv, valid=None):
    steps, rows, chans = steady.shape
    for start in range(0, rows, 16):
        block = block_ref[start : start + 16].astype(F32)
        if valid is not None:
            block = jnp.where(valid, block, 0.0)
        steady[:, start : start + 16] = jnp.swapaxes(block, 0, 1).astype(BF)
        yield
    wout = doubled(wout)
    for s in range(0, steps, 8):
        for t, piece in enumerate(two_halves(steady[s : s + 8], wout, ((1,), (1,)))):
            conv[s + t] = piece.astype(BF)
        yield
    for s in range(0, steps, 2):
        part[s // 2, :, 0:rows] = steady[s].T
        part[s // 2, :, rows : 2 * rows] = steady[s + 1].T
        yield


def take_block(*args):
    for _ in block_steps(*args):
        pass


def place_part(part, cross_ref, slot, sem):
    size = part.shape[0]
    copy = pltpu.make_async_copy(part, cross_ref.at[pl.ds(slot * size, size)], sem)
    copy.start()
    return copy


def add_lags(sums, conv, lags_ref, base, where, causal):
    steps = conv.shape[0]
    for t in range(steps):
        value = conv[t, where, :].astype(F32)
        for s in range(steps):
            if causal and t < s:
                continue
            tap = lags_ref[base + (t - s)]
            sums[s][0] += tap * value[:8]
            sums[s][1] += tap * value[8:]


def early_body(
    ids_src, coup_src, cot_src, taps_src, wout_src, wg_src, near_ref,
    sum_ref, cross_ref, mix_ref, mixt_ref, steady_ref, taps_ref, wout_ref, wg_ref, lags_ref,
    part, conv, other, other_part, other_conv, dense, coup_ref, cot_ref, ids_ref, sems,
):
    copies = load_all(
        sems,
        [
            (cot_src, cot_ref), (wout_src, wout_ref), (taps_src, taps_ref),
            (coup_src, coup_ref), (wg_src, wg_ref), (ids_src, ids_ref),
        ],
    )
    for copy in copies:
        copy.wait()
    rows, steps, chans = cot_ref.shape
    blocks, slots, half = coup_ref.shape[:3]
    bus = lax.axis_index("bus")
    first = bus * blocks - 1
    turned = (bus & 1) == 0
    odd = lax.axis_index("tm") & 1
    take_block(cot_ref, wout_ref[...], steady_ref, part, conv)
    sent = [place_part(part, cross_ref, 0, sems.at[6])]
    take_block(near_ref, wout_ref[...], other, other_part, other_conv, odd == 0)
    sent.append(place_part(other_part, cross_ref, 1 + 2 * odd, sems.at[7]))
    taps = taps_ref[...].astype(F32)
    for lag in range(taps_ref.shape[0]):
        lags_ref[lag] = jnp.broadcast_to(taps[lag : lag + 1], (8, chans))

    def tile(index, carry):
        where = pl.ds(pl.multiple_of(index * 16, 16), 16)
        sums = [[jnp.zeros((8, chans), F32)] * 2 for _ in range(steps)]
        add_lags(sums, conv, lags_ref, 0, where, True)
        add_lags(sums, other_conv, lags_ref, steps, where, False)
        for s in range(steps):
            sum_ref[s, where, :] = jnp.concatenate(sums[s], axis=0)
        return carry

    lax.fori_loop(0, rows // 16, tile, 0)
    dense[...] = jnp.zeros_like(dense)
    for i in range(blocks):
        for k in range(slots):
            place = ids_ref[i, k] - first
            place = jnp.where(turned, blocks + 1 - place, place)
            dense[i, place] += coup_ref[i, k].astype(F32)
    full = jnp.concatenate(
        [
            jnp.concatenate([dense[i, j] for j in range(blocks + 2)], axis=1)
            for i in range(blocks)
        ],
        axis=0,
    )
    mix_ref[...] = full.astype(BF)
    mixt_ref[...] = full.T.astype(BF)
    for copy in sent:
        copy.wait()


def far_body(sum_ref, crossed_ref, block_ref, lags_ref, wout_ref, out_ref, cross_ref, steady, part, conv, sems):
    steps, rows, chans = conv.shape
    valid = lax.axis_index("tm") < 2

    @pl.when(valid)
    def _():
        take_block(block_ref, wout_ref[...], steady, part, conv)
        sent = place_part(part, cross_ref, 2, sems.at[0])

        def tile(index, carry):
            where = pl.ds(pl.multiple_of(index * 16, 16), 16)
            sums = [[sum_ref[s, where, :][:8], sum_ref[s, where, :][8:]] for s in range(steps)]
            add_lags(sums, conv, lags_ref, 2 * steps, where, False)
            for s in range(steps):
                out_ref[s, where, :] = jnp.concatenate(sums[s], axis=0)
            return carry

        lax.fori_loop(0, rows // 16, tile, 0)
        sent.wait()

    @pl.when(jnp.logical_not(valid))
    def _():
        part[...] = jnp.zeros_like(part)
        sent = place_part(part, cross_ref, 2, sems.at[0])
        out_ref[...] = sum_ref[...]
        sent.wait()


def lag_steps(sum_ref, conv, lags, base, grad_ref, start):
    steps = grad_ref.shape[0]
    where = slice(start, start + 16)
    sums = []
    for s in range(steps):
        value = sum_ref[s, where, :]
        sums.append([value[:8], value[8:]])
    for t in range(steps):
        value = conv[t, where, :].astype(F32)
        for s in range(steps):
            tap = lags[base + (t - s)]
            sums[s][0] += tap * value[:8]
            sums[s][1] += tap * value[8:]
        yield
    for s in range(steps):
        grad_ref[s, where, :] = jnp.concatenate(sums[s], axis=0).astype(BF)
    yield


def tail_body(
    even_own, odd_own, even_ref, odd_ref, mix_ref, mixt_ref, wg_ref, wout_ref, taps_ref, lags_ref,
    sum_ref, swapped_ref, crossed_ref, mark_ref,
    keep_ref, send_ref, mixed_out, even_out, odd_out,
    slope_ref, mixed_ref, stack, steady, conv, cross, window, grad_ref, pack, sems,
):
    steps, rows, chans = mixed_ref.shape
    half = even_ref.shape[1]
    pairs = cross.shape[0]
    tm = lax.axis_index("tm")
    odd = tm & 1
    block = steps // 2
    near_at, slot = 1 + 2 * odd, 3 - 2 * odd
    copies = []
    for i, at in enumerate((0, near_at, 2)):
        where = pl.ds(at * block, block)
        copies.append(pltpu.make_async_copy(crossed_ref.at[where], cross.at[where], sems.at[i]))
        copies[-1].start()

    group = 4
    mix, wg = mix_ref[...], doubled(wg_ref[...])
    zero = jnp.zeros((rows, chans), BF)
    other = block_steps(
        swapped_ref, wout_ref[...], steady, cross.at[pl.ds(slot * block, block)], conv, tm < 2
    )
    stack[0, 0:rows, chans : 2 * chans] = zero
    stack[block, 0:rows, chans : 2 * chans] = zero
    stack[block, rows : 2 * rows, 0:chans] = zero
    wide_group = 2 * group
    for s in range(0, steps, wide_group):
        mixed = []
        for start in range(s, s + wide_group, group):
            ext = jnp.concatenate(
                [
                    jnp.concatenate([even_ref[t], even_own[t], odd_own[t], odd_ref[t]], axis=0)
                    for t in range(start, start + group)
                ],
                axis=1,
            )
            found = dot(mix, ext).astype(BF)
            mixed += [found[:, t * chans : (t + 1) * chans] for t in range(group)]
            next(other, None)
        mixed = jnp.stack(mixed)
        mixed_ref[s : s + wide_group] = mixed
        for t, pre in enumerate(two_halves(mixed, wg), s):
            gate = 0.5 + 0.5 * jnp.tanh(0.5 * pre)
            act = (pre * gate).astype(BF)
            slope_ref[t] = gate * (1.0 + pre * (1.0 - gate))
            low = (t % 2) * rows
            stack[t // 2, low : low + rows, 0:chans] = act
            low = ((t + 1) % 2) * rows if t < steps - 1 else rows
            stack[(t + 1) // 2, low : low + rows, chans : 2 * chans] = act
            if t == steps - 1:
                stack[block, 0:rows, 0:chans] = act
            next(other, None)
    for _ in other:
        pass
    window[0:31] = lags_ref[pl.ds(slot * steps - 15, 31)]
    for copy in copies:
        copy.wait()

    weight = wout_ref[...].astype(F32).T
    taps = taps_ref[...].astype(F32)
    out_at, lag_at = chans, 2 * chans

    def lag_group(at, tiles):
        work = itertools.chain.from_iterable(
            [lag_steps(sum_ref, conv, window, 15, grad_ref, tile) for tile in tiles]
        )
        totals = []
        for first in (at, at + group):
            total = [None] * group
            for i in range(block):
                count = min(group, pairs - first - i)
                if count > 0:
                    left = cross[first + i : first + i + count].reshape(count * rows, 2 * rows)
                    part = dot(left, stack[i])
                    for g in range(count):
                        piece = part[g * rows : (g + 1) * rows]
                        total[g] = piece if total[g] is None else total[g] + piece
                for _ in range(5):
                    next(work, None)
            totals.append(total)
        for _ in work:
            pass
        last = None
        if at + 2 * group + block <= pairs:
            left = jnp.concatenate(
                [
                    cross[first + block : first + block + group, :, 0:rows].reshape(
                        group * rows, rows
                    )
                    for first in (at, at + group)
                ],
                axis=1,
            )
            last = dot(left, stack[block])
        out, found = jnp.zeros((chans, chans), F32), []
        for half_at, total in enumerate(totals):
            for g in range(group):
                for side in range(2):
                    lag = 2 * (at + half_at * group + g) + side
                    part = total[g][:, side * chans : (side + 1) * chans]
                    if side == 1 and last is not None:
                        lanes = slice(half_at * chans, (half_at + 1) * chans)
                        part = part + last[g * rows : (g + 1) * rows, lanes]
                    out += part * taps[lag : lag + 1]
                    found.append(jnp.sum(part * weight, axis=0, keepdims=True))
        pack[lag_at + 2 * at : lag_at + 2 * (at + 2 * group)] = jnp.concatenate(found, axis=0)
        return out

    middle = pairs // 2
    out = jnp.zeros((chans, chans), F32)
    for at in range(0, middle, 2 * group):
        out += lag_group(at, range(at * 8, at * 8 + 64, 16))
    pack[out_at:lag_at] = out

    @pl.when(tm < 2)
    def _():
        out = pack[out_at:lag_at]
        for at in range(middle, pairs, 2 * group):
            out += lag_group(at, ())
        pack[out_at:lag_at] = out

    @pl.when(tm >= 2)
    def _():
        pack[lag_at + 2 * middle :] = jnp.zeros((2 * (pairs - middle), chans), F32)

    mixt = jnp.concatenate([mixt_ref[:half], mixt_ref[half + rows :]], axis=0)
    graph = jnp.zeros((chans, chans), F32)
    for s in range(0, steps, wide_group):
        grad = grad_ref[s : s + wide_group].astype(F32) * slope_ref[s : s + wide_group]
        grad_pre = grad.astype(BF)
        flat = (wide_group * rows, chans)
        mixed = mixed_ref[s : s + wide_group].reshape(flat)
        graph += dot(mixed, grad_pre.reshape(flat), ((0,), (0,)))
        grad_mixed = [piece.astype(BF) for piece in two_halves(grad_pre, wg, ((1,), (1,)))]
        for start in range(0, wide_group, group):
            spread = dot(mixt, jnp.concatenate(grad_mixed[start : start + group], axis=1))
            for t in range(group):
                part = spread[:, t * chans : (t + 1) * chans]
                even_out[s + start + t] = part[:half].astype(BF)
                odd_out[s + start + t] = part[half:].astype(BF)
                mixed_out[s + start + t] = grad_mixed[start + t]

    pack[0:chans] = graph
    pack[out_at:lag_at] = pack[out_at:lag_at].T
    size = keep_ref.shape[0]
    keep_ref[...] = pack[pl.ds(pl.multiple_of(odd * size, size), size)]
    send_ref[...] = pack[pl.ds(pl.multiple_of((1 - odd) * size, size), size)]


def mark_body(first_ref, second_ref, mark_ref):
    mark_ref[...] = first_ref[0, 0:8].astype(F32) + second_ref[0, 0:8].astype(F32)


def fold_body(grad_ref, mixt_ref, cot_ref, out_ref):
    steps, rows, chans = grad_ref.shape
    half = rows // 2
    odd = lax.axis_index("bus") & 1
    low, high = pl.multiple_of(odd * half, half), pl.multiple_of((1 - odd) * half, half)
    mixt = mixt_ref[half : half + rows]
    for s in range(0, steps, 4):
        grads = jnp.concatenate([grad_ref[t] for t in range(s, s + 4)], axis=1)
        spread = dot(mixt, grads)
        for t in range(4):
            part = spread[:, t * chans : (t + 1) * chans]
            out_ref[s + t, :half] = part[:half] + cot_ref[s + t, pl.ds(high, half)].astype(F32)
            out_ref[s + t, half:] = part[half:] + cot_ref[s + t, pl.ds(low, half)].astype(F32)


def edge_add_body(spread_ref, even_ref, out_ref):
    half = even_ref.shape[1]
    for s in range(spread_ref.shape[0]):
        out_ref[s, :half] = spread_ref[s, :half] + even_ref[s].astype(F32)
        out_ref[s, half:] = spread_ref[s, half:]


def final_body(spread_ref, odd_ref, out_ref):
    half = odd_ref.shape[1]
    odd = lax.axis_index("bus") & 1
    for start in range(0, half, 16):
        part = spread_ref[:, start : start + 16]
        where = pl.ds((1 - odd) * half + start, 16)
        out_ref[where] = jnp.swapaxes(part, 0, 1).astype(BF)
        part = spread_ref[:, half + start : half + start + 16]
        part = part + odd_ref[:, start : start + 16].astype(F32)
        where = pl.ds(odd * half + start, 16)
        out_ref[where] = jnp.swapaxes(part, 0, 1).astype(BF)


def pause_body(value_ref, last_ref, out_ref):
    out_ref[...] = value_ref[0:8] + last_ref[...]


def finish_body(scale, mine_ref, other_ref, mark_ref, graph_ref, out_ref, taps_ref, pack):
    odd = lax.axis_index("tm") & 1
    size = mine_ref.shape[0]
    chans = graph_ref.shape[0]
    pack[pl.ds(pl.multiple_of(odd * size, size), size)] = mine_ref[...] * scale
    pack[pl.ds(pl.multiple_of((1 - odd) * size, size), size)] = other_ref[...] * scale
    graph_ref[...] = pack[0:chans]
    out_ref[...] = pack[chans : 2 * chans]
    taps_ref[...] = pack[2 * chans :]


def swap(value, axis, distance):
    size = lax.axis_size(axis)
    return lax.ppermute(value, axis, [(i, i ^ distance) for i in range(size)])


def pause(value, received, mark):
    (mark,) = call(pause_body, [(mark.shape, F32)], value, mark, cost=1 << 36)
    return lax.optimization_barrier((received, mark))


def shards(features, couplings, neighbors, w_graph, kernel_taps, w_out, cotangent):
    bus, tm = lax.axis_size("bus"), lax.axis_size("tm")
    rows, steps, chans = features.shape
    blocks, slots, half = couplings.shape[:3]
    total = kernel_taps.shape[0]
    evens = [(i, i ^ 1) for i in range(bus)]
    odds = [(i, i + 1) for i in range(1, bus - 1, 2)] + [(i + 1, i) for i in range(1, bus - 1, 2)]
    odds += [(0, 0), (bus - 1, bus - 1)]
    wide = (steps, rows, chans)
    edge = (steps, half, chans)
    square = (chans, chans)

    def edge_of(even):
        (found,) = call(
            functools.partial(edge_body, even), [(edge, BF)], features,
            scratch=[
                pltpu.VMEM((half,) + features.shape[1:], BF), pltpu.SemaphoreType.DMA((half // 16,))
            ],
            far=[0],
        )
        return found

    even_own, odd_own = edge_of(True), edge_of(False)
    near = swap(cotangent, "tm", 1)
    odd_edge = lax.ppermute(odd_own, "bus", odds)
    even_edge = lax.ppermute(even_own, "bus", evens)
    far = swap(cotangent, "tm", 2)

    pairs = total // 2
    crossing = (pairs, chans, 2 * rows)
    ext = rows + 2 * half
    part = pltpu.VMEM((steps // 2, chans, 2 * rows), BF)
    sums, crossed, mix, mixt, steady, taps, wout, wg, lags = call(
        early_body,
        [
            (wide, F32), (crossing, BF), ((rows, ext), BF), ((ext, rows), BF), (wide, BF),
            (kernel_taps.shape, BF), (square, BF), (square, BF), ((total, 8, chans), F32),
        ],
        neighbors, couplings, cotangent, kernel_taps, w_out, w_graph, near,
        scratch=[
            part, pltpu.VMEM(wide, BF), pltpu.VMEM(wide, BF), part, pltpu.VMEM(wide, BF),
            pltpu.VMEM((blocks, blocks + 2, half, half), F32),
            pltpu.VMEM(couplings.shape, BF),
            pltpu.VMEM(cotangent.shape, BF),
            pltpu.SMEM(neighbors.shape, jnp.int32),
            pltpu.SemaphoreType.DMA((8,)),
        ],
        far=range(6), kept=(None, 1),
    )

    far, sums = lax.optimization_barrier((far, sums))
    swapped = swap(far, "tm", 1)
    sums, crossed = call(
        far_body, [(wide, F32), (crossing, BF)], sums, crossed, far, lags, wout,
        scratch=[
            pltpu.VMEM(wide, BF), part, pltpu.VMEM(wide, BF), pltpu.SemaphoreType.DMA((1,))
        ],
        kept=(1, 1),
    )
    even_edge, odd_edge, sums = lax.optimization_barrier((even_edge, odd_edge, sums))
    (mark,) = call(mark_body, [((8, chans), F32)], even_edge, odd_edge, cost=1 << 36)
    swapped, mark = lax.optimization_barrier((swapped, mark))
    size = (2 * chans + total) // 2
    keep, send, grad_mixed, even_grad, odd_grad = call(
        tail_body,
        [((size, chans), F32), ((size, chans), F32), (wide, BF), (edge, BF), (edge, BF)],
        even_own, odd_own, even_edge, odd_edge, mix, mixt, wg, wout, taps, lags,
        sums, swapped, crossed, mark,
        scratch=[
            pltpu.VMEM(wide, F32), pltpu.VMEM(wide, BF),
            pltpu.VMEM((steps // 2 + 1, 2 * rows, 2 * chans), BF),
            pltpu.VMEM(wide, BF), pltpu.VMEM(wide, BF), pltpu.VMEM(crossing, BF),
            pltpu.VMEM((32, 8, chans), F32), pltpu.VMEM(wide, BF),
            pltpu.VMEM((2 * size, chans), F32), pltpu.SemaphoreType.DMA((3,)),
        ],
        anywhere=[12],
    )
    mark = send[0:8]
    odd_grad = lax.ppermute(odd_grad, "bus", evens)
    keep = keep + swap(send, "tm", 1)
    keep, even_grad = lax.optimization_barrier((keep, even_grad))
    even_grad = lax.ppermute(even_grad, "bus", evens)
    hops = [("bus", 1 << bit) for bit in range(1, bus.bit_length() - 1)]
    hops += [("tm", 1 << bit) for bit in range(1, tm.bit_length() - 1)] + [("bus", 1)]
    onward = [(i, i + 2) for i in range(0, bus - 2, 2)] + [(i, i - 2) for i in range(3, bus, 2)]
    for place, (axis, distance) in enumerate(hops):
        sent = keep.astype(BF)
        received = swap(sent, axis, distance)
        if place < len(hops) - 2:
            received, mark = pause(keep, received, mark)
            if place == 0:
                odd_grad, mark = lax.optimization_barrier((odd_grad, mark))
                odd_grad = lax.ppermute(odd_grad, "bus", onward)
        elif place == len(hops) - 2:
            (spread,) = call(
                fold_body, [(wide, F32)], grad_mixed, mixt, steady, cost=1 << 36
            )
            received, spread = lax.optimization_barrier((received, spread))
        else:
            (spread,) = call(edge_add_body, [(wide, F32)], spread, even_grad, cost=1 << 36)
            received, spread = lax.optimization_barrier((received, spread))
        keep = sent.astype(F32) + received.astype(F32)
    other = swap(keep, "tm", 1)
    (grad_features,) = call(
        final_body, [(features.shape, BF)], spread, odd_grad, cost=1 << 36
    )
    other, grad_features = lax.optimization_barrier((other, grad_features))
    scale = 1.0 / math.sqrt(bus * rows * steps * tm)
    grad_graph, grad_out, grad_taps = call(
        functools.partial(finish_body, scale),
        [(square, F32), (square, F32), ((total, chans), F32)],
        keep, other, mark,
        scratch=[pltpu.VMEM((2 * size, chans), F32)],
    )
    return grad_features, grad_graph, grad_out, grad_taps


def solution(mesh):
    return jax.shard_map(
        shards,
        mesh=mesh,
        in_specs=(
            P("bus", "tm", None),
            P("bus", None, None, None),
            P("bus", None),
            P(),
            P(),
            P(),
            P("bus", "tm", None),
        ),
        out_specs=(P("bus", "tm", None), P(), P(), P()),
        check_vma=False,
    )
```

```python
import functools
import itertools
import math

import jax
import jax.numpy as jnp
from jax import lax
from jax.experimental import pallas as pl
from jax.experimental.pallas import tpu as pltpu
from jax.sharding import PartitionSpec as P

BF = jnp.bfloat16
F32 = jnp.float32
VMEM = pl.BlockSpec(memory_space=pltpu.VMEM)
LIMIT = 16 << 20


def call(body, outs, *args, scratch=(), far=(), cost=1, kept=None, anywhere=(), placed=True):
    specs = [VMEM] * len(args)
    results = [VMEM if placed else pl.BlockSpec(memory_space=pl.ANY)] * len(outs)
    args = list(args)
    for i in anywhere:
        specs[i] = pl.BlockSpec(memory_space=pl.ANY)
    aliases = {}
    if kept is not None:
        results[kept[1]] = pl.BlockSpec(memory_space=pl.ANY)
        if kept[0] is not None:
            specs[kept[0]] = pl.BlockSpec(memory_space=pl.ANY)
            aliases = {kept[0]: kept[1]}
    for i in far:
        specs[i] = pl.BlockSpec(memory_space=pltpu.HBM)
        args[i] = pltpu.with_memory_space_constraint(args[i], pltpu.HBM)
    return pl.pallas_call(
        body,
        out_shape=[jax.ShapeDtypeStruct(shape, dtype) for shape, dtype in outs],
        in_specs=specs,
        out_specs=results,
        input_output_aliases=aliases,
        scratch_shapes=list(scratch),
        compiler_params=pltpu.CompilerParams(vmem_limit_bytes=LIMIT),
        cost_estimate=pl.CostEstimate(flops=cost, bytes_accessed=1, transcendentals=0),
    )(*args)


def dot(left, right, dims=((1,), (0,))):
    return lax.dot_general(left, right, (dims, ((), ())), preferred_element_type=F32)


def doubled(weight):
    zero = jnp.zeros_like(weight)
    top = jnp.concatenate([weight, zero], axis=1)
    return jnp.concatenate([top, jnp.concatenate([zero, weight], axis=1)], axis=0)


def two_halves(values, weight, dims=((1,), (0,))):
    count, rows, chans = values.shape
    flat = values.reshape(count * rows, chans)
    middle = count * rows // 2
    both = dot(jnp.concatenate([flat[:middle], flat[middle:]], axis=1), weight, dims)
    return [
        both[t * rows : (t + 1) * rows, h * chans : (h + 1) * chans]
        for h in range(2)
        for t in range(count // 2)
    ]


def load_all(sems, pairs):
    copies = [
        pltpu.make_async_copy(source, target, sems.at[i])
        for i, (source, target) in enumerate(pairs)
    ]
    for copy in copies:
        copy.start()
    return copies


def edge_body(even, source_ref, edge_ref, feat_ref, sems):
    half = feat_ref.shape[0]
    odd = lax.axis_index("bus") & 1
    first = pl.multiple_of((1 - odd if even else odd) * half, half)
    copies = load_all(
        sems,
        [
            (source_ref.at[pl.ds(first + start, 16)], feat_ref.at[pl.ds(start, 16)])
            for start in range(0, half, 16)
        ],
    )
    for copy, start in zip(copies, range(0, half, 16)):
        copy.wait()
        edge_ref[:, start : start + 16] = jnp.swapaxes(
            feat_ref[start : start + 16].astype(F32), 0, 1
        ).astype(BF)


def block_steps(block_ref, wout, steady, part, conv, valid=None):
    steps, rows, chans = steady.shape
    for start in range(0, rows, 16):
        block = block_ref[start : start + 16].astype(F32)
        if valid is not None:
            block = jnp.where(valid, block, 0.0)
        steady[:, start : start + 16] = jnp.swapaxes(block, 0, 1).astype(BF)
        yield
    wout = doubled(wout)
    for s in range(0, steps, 8):
        for t, piece in enumerate(two_halves(steady[s : s + 8], wout, ((1,), (1,)))):
            conv[s + t] = piece.astype(BF)
        yield
    for s in range(0, steps, 2):
        part[s // 2, :, 0:rows] = steady[s].T
        part[s // 2, :, rows : 2 * rows] = steady[s + 1].T
        yield


def take_block(*args):
    for _ in block_steps(*args):
        pass


def place_part(part, cross_ref, slot, sem):
    size = part.shape[0]
    copy = pltpu.make_async_copy(part, cross_ref.at[pl.ds(slot * size, size)], sem)
    copy.start()
    return copy


def add_lags(sums, conv, lags_ref, base, where, causal):
    steps = conv.shape[0]
    for t in range(steps):
        value = conv[t, where, :].astype(F32)
        for s in range(steps):
            if causal and t < s:
                continue
            tap = lags_ref[base + (t - s)]
            sums[s][0] += tap * value[:8]
            sums[s][1] += tap * value[8:]


def early_body(
    ids_src, coup_src, cot_src, taps_src, wout_src, wg_src, near_ref,
    sum_ref, cross_ref, mix_ref, mixt_ref, steady_ref, taps_ref, wout_ref, wg_ref, lags_ref,
    part, conv, other, other_part, other_conv, dense, coup_ref, cot_ref, ids_ref, sems,
):
    copies = load_all(
        sems,
        [
            (cot_src, cot_ref), (wout_src, wout_ref), (taps_src, taps_ref),
            (coup_src, coup_ref), (wg_src, wg_ref), (ids_src, ids_ref),
        ],
    )
    for copy in copies:
        copy.wait()
    rows, steps, chans = cot_ref.shape
    blocks, slots, half = coup_ref.shape[:3]
    bus = lax.axis_index("bus")
    first = bus * blocks - 1
    turned = (bus & 1) == 0
    odd = lax.axis_index("tm") & 1
    take_block(cot_ref, wout_ref[...], steady_ref, part, conv)
    sent = [place_part(part, cross_ref, 0, sems.at[6])]
    take_block(near_ref, wout_ref[...], other, other_part, other_conv, odd == 0)
    sent.append(place_part(other_part, cross_ref, 1 + 2 * odd, sems.at[7]))
    taps = taps_ref[...].astype(F32)
    for lag in range(taps_ref.shape[0]):
        lags_ref[lag] = jnp.broadcast_to(taps[lag : lag + 1], (8, chans))

    def tile(index, carry):
        where = pl.ds(pl.multiple_of(index * 16, 16), 16)
        sums = [[jnp.zeros((8, chans), F32)] * 2 for _ in range(steps)]
        add_lags(sums, conv, lags_ref, 0, where, True)
        add_lags(sums, other_conv, lags_ref, steps, where, False)
        for s in range(steps):
            sum_ref[s, where, :] = jnp.concatenate(sums[s], axis=0)
        return carry

    lax.fori_loop(0, rows // 16, tile, 0)
    dense[...] = jnp.zeros_like(dense)
    for i in range(blocks):
        for k in range(slots):
            place = ids_ref[i, k] - first
            place = jnp.where(turned, blocks + 1 - place, place)
            dense[i, place] += coup_ref[i, k].astype(F32)
    full = jnp.concatenate(
        [
            jnp.concatenate([dense[i, j] for j in range(blocks + 2)], axis=1)
            for i in range(blocks)
        ],
        axis=0,
    )
    mix_ref[...] = full.astype(BF)
    mixt_ref[...] = full.T.astype(BF)
    for copy in sent:
        copy.wait()


def far_body(sum_ref, crossed_ref, block_ref, lags_ref, wout_ref, out_ref, cross_ref, steady, part, conv, sems):
    steps, rows, chans = conv.shape
    valid = lax.axis_index("tm") < 2

    @pl.when(valid)
    def _():
        take_block(block_ref, wout_ref[...], steady, part, conv)
        sent = place_part(part, cross_ref, 2, sems.at[0])

        def tile(index, carry):
            where = pl.ds(pl.multiple_of(index * 16, 16), 16)
            sums = [[sum_ref[s, where, :][:8], sum_ref[s, where, :][8:]] for s in range(steps)]
            add_lags(sums, conv, lags_ref, 2 * steps, where, False)
            for s in range(steps):
                out_ref[s, where, :] = jnp.concatenate(sums[s], axis=0)
            return carry

        lax.fori_loop(0, rows // 16, tile, 0)
        sent.wait()

    @pl.when(jnp.logical_not(valid))
    def _():
        part[...] = jnp.zeros_like(part)
        sent = place_part(part, cross_ref, 2, sems.at[0])
        out_ref[...] = sum_ref[...]
        sent.wait()


def lag_steps(sum_ref, conv, lags, base, grad_ref, start):
    steps = grad_ref.shape[0]
    where = slice(start, start + 16)
    sums = []
    for s in range(steps):
        value = sum_ref[s, where, :]
        sums.append([value[:8], value[8:]])
    for t in range(steps):
        value = conv[t, where, :].astype(F32)
        for s in range(steps):
            tap = lags[base + (t - s)]
            sums[s][0] += tap * value[:8]
            sums[s][1] += tap * value[8:]
        yield
    for s in range(steps):
        grad_ref[s, where, :] = jnp.concatenate(sums[s], axis=0).astype(BF)
    yield


def tail_body(
    even_own, odd_own, even_ref, odd_ref, mix_ref, mixt_ref, wg_ref, wout_ref, taps_ref, lags_ref,
    sum_ref, swapped_ref, crossed_ref, mark_ref,
    keep_ref, send_ref, mixed_out, even_out, odd_out,
    slope_ref, mixed_ref, stack, steady, conv, cross, window, grad_ref, pack, sems,
):
    steps, rows, chans = mixed_ref.shape
    half = even_ref.shape[1]
    pairs = cross.shape[0]
    tm = lax.axis_index("tm")
    odd = tm & 1
    block = steps // 2
    near_at, slot = 1 + 2 * odd, 3 - 2 * odd
    copies = []
    for i, at in enumerate((0, near_at, 2)):
        where = pl.ds(at * block, block)
        copies.append(pltpu.make_async_copy(crossed_ref.at[where], cross.at[where], sems.at[i]))
        copies[-1].start()

    group = 4
    mix, wg = mix_ref[...], doubled(wg_ref[...])
    zero = jnp.zeros((rows, chans), BF)
    other = block_steps(
        swapped_ref, wout_ref[...], steady, cross.at[pl.ds(slot * block, block)], conv, tm < 2
    )
    stack[0, 0:rows, chans : 2 * chans] = zero
    stack[block, 0:rows, chans : 2 * chans] = zero
    stack[block, rows : 2 * rows, 0:chans] = zero
    wide_group = 2 * group
    for s in range(0, steps, wide_group):
        mixed = []
        for start in range(s, s + wide_group, group):
            ext = jnp.concatenate(
                [
                    jnp.concatenate([even_ref[t], even_own[t], odd_own[t], odd_ref[t]], axis=0)
                    for t in range(start, start + group)
                ],
                axis=1,
            )
            found = dot(mix, ext).astype(BF)
            mixed += [found[:, t * chans : (t + 1) * chans] for t in range(group)]
            next(other, None)
        mixed = jnp.stack(mixed)
        mixed_ref[s : s + wide_group] = mixed
        for t, pre in enumerate(two_halves(mixed, wg), s):
            gate = 0.5 + 0.5 * jnp.tanh(0.5 * pre)
            act = (pre * gate).astype(BF)
            slope_ref[t] = gate * (1.0 + pre * (1.0 - gate))
            low = (t % 2) * rows
            stack[t // 2, low : low + rows, 0:chans] = act
            low = ((t + 1) % 2) * rows if t < steps - 1 else rows
            stack[(t + 1) // 2, low : low + rows, chans : 2 * chans] = act
            if t == steps - 1:
                stack[block, 0:rows, 0:chans] = act
            next(other, None)
    for _ in other:
        pass
    window[0:31] = lags_ref[pl.ds(slot * steps - 15, 31)]
    for copy in copies:
        copy.wait()

    weight = wout_ref[...].astype(F32).T
    taps = taps_ref[...].astype(F32)
    out_at, lag_at = chans, 2 * chans

    def lag_group(at, tiles):
        work = itertools.chain.from_iterable(
            [lag_steps(sum_ref, conv, window, 15, grad_ref, tile) for tile in tiles]
        )
        totals = []
        for first in (at, at + group):
            total = [None] * group
            for i in range(block):
                count = min(group, pairs - first - i)
                if count > 0:
                    left = cross[first + i : first + i + count].reshape(count * rows, 2 * rows)
                    part = dot(left, stack[i])
                    for g in range(count):
                        piece = part[g * rows : (g + 1) * rows]
                        total[g] = piece if total[g] is None else total[g] + piece
                for _ in range(5):
                    next(work, None)
            totals.append(total)
        for _ in work:
            pass
        last = None
        if at + 2 * group + block <= pairs:
            left = jnp.concatenate(
                [
                    cross[first + block : first + block + group, :, 0:rows].reshape(
                        group * rows, rows
                    )
                    for first in (at, at + group)
                ],
                axis=1,
            )
            last = dot(left, stack[block])
        out, found = jnp.zeros((chans, chans), F32), []
        for half_at, total in enumerate(totals):
            for g in range(group):
                for side in range(2):
                    lag = 2 * (at + half_at * group + g) + side
                    part = total[g][:, side * chans : (side + 1) * chans]
                    if side == 1 and last is not None:
                        lanes = slice(half_at * chans, (half_at + 1) * chans)
                        part = part + last[g * rows : (g + 1) * rows, lanes]
                    out += part * taps[lag : lag + 1]
                    found.append(jnp.sum(part * weight, axis=0, keepdims=True))
        pack[lag_at + 2 * at : lag_at + 2 * (at + 2 * group)] = jnp.concatenate(found, axis=0)
        return out

    middle = pairs // 2
    out = jnp.zeros((chans, chans), F32)
    for at in range(0, middle, 2 * group):
        out += lag_group(at, range(at * 8, at * 8 + 64, 16))
    pack[out_at:lag_at] = out

    @pl.when(tm < 2)
    def _():
        out = pack[out_at:lag_at]
        for at in range(middle, pairs, 2 * group):
            out += lag_group(at, ())
        pack[out_at:lag_at] = out

    @pl.when(tm >= 2)
    def _():
        pack[lag_at + 2 * middle :] = jnp.zeros((2 * (pairs - middle), chans), F32)

    mixt = jnp.concatenate([mixt_ref[:half], mixt_ref[half + rows :]], axis=0)
    graph = jnp.zeros((chans, chans), F32)
    for s in range(0, steps, wide_group):
        grad = grad_ref[s : s + wide_group].astype(F32) * slope_ref[s : s + wide_group]
        grad_pre = grad.astype(BF)
        flat = (wide_group * rows, chans)
        mixed = mixed_ref[s : s + wide_group].reshape(flat)
        graph += dot(mixed, grad_pre.reshape(flat), ((0,), (0,)))
        grad_mixed = [piece.astype(BF) for piece in two_halves(grad_pre, wg, ((1,), (1,)))]
        for start in range(0, wide_group, group):
            spread = dot(mixt, jnp.concatenate(grad_mixed[start : start + group], axis=1))
            for t in range(group):
                part = spread[:, t * chans : (t + 1) * chans]
                even_out[s + start + t] = part[:half].astype(BF)
                odd_out[s + start + t] = part[half:].astype(BF)
                mixed_out[s + start + t] = grad_mixed[start + t]

    pack[0:chans] = graph
    pack[out_at:lag_at] = pack[out_at:lag_at].T
    size = keep_ref.shape[0]
    keep_ref[...] = pack[pl.ds(pl.multiple_of(odd * size, size), size)]
    send_ref[...] = pack[pl.ds(pl.multiple_of((1 - odd) * size, size), size)]


def mark_body(first_ref, second_ref, mark_ref):
    mark_ref[...] = first_ref[0, 0:8].astype(F32) + second_ref[0, 0:8].astype(F32)


def fold_body(grad_ref, mixt_ref, cot_ref, out_ref):
    steps, rows, chans = grad_ref.shape
    half = rows // 2
    odd = lax.axis_index("bus") & 1
    low, high = pl.multiple_of(odd * half, half), pl.multiple_of((1 - odd) * half, half)
    mixt = mixt_ref[half : half + rows]
    for s in range(0, steps, 4):
        grads = jnp.concatenate([grad_ref[t] for t in range(s, s + 4)], axis=1)
        spread = dot(mixt, grads)
        for t in range(4):
            part = spread[:, t * chans : (t + 1) * chans]
            out_ref[s + t, :half] = part[:half] + cot_ref[s + t, pl.ds(high, half)].astype(F32)
            out_ref[s + t, half:] = part[half:] + cot_ref[s + t, pl.ds(low, half)].astype(F32)


def edge_add_body(spread_ref, even_ref, out_ref):
    half = even_ref.shape[1]
    for s in range(spread_ref.shape[0]):
        out_ref[s, :half] = spread_ref[s, :half] + even_ref[s].astype(F32)
        out_ref[s, half:] = spread_ref[s, half:]


def final_body(spread_ref, odd_ref, out_ref):
    half = odd_ref.shape[1]
    odd = lax.axis_index("bus") & 1
    for start in range(0, half, 16):
        part = spread_ref[:, start : start + 16]
        where = pl.ds((1 - odd) * half + start, 16)
        out_ref[where] = jnp.swapaxes(part, 0, 1).astype(BF)
        part = spread_ref[:, half + start : half + start + 16]
        part = part + odd_ref[:, start : start + 16].astype(F32)
        where = pl.ds(odd * half + start, 16)
        out_ref[where] = jnp.swapaxes(part, 0, 1).astype(BF)


def pause_body(value_ref, last_ref, out_ref):
    out_ref[...] = value_ref[0:8] + last_ref[...]


def finish_body(mine_ref, other_ref, mark_ref, graph_ref, out_ref, taps_ref, sems):
    size = mine_ref.shape[0]
    chans = graph_ref.shape[0]
    extra = size - chans
    odd = lax.axis_index("tm") & 1
    for side, low, high in ((0, mine_ref, other_ref), (1, other_ref, mine_ref)):

        @pl.when(odd == side)
        def _():
            copies = load_all(
                sems,
                [
                    (low.at[pl.ds(0, chans)], graph_ref),
                    (low.at[pl.ds(chans, extra)], out_ref.at[pl.ds(0, extra)]),
                    (high.at[pl.ds(0, chans - extra)], out_ref.at[pl.ds(extra, chans - extra)]),
                    (high.at[pl.ds(chans - extra, size - chans + extra)], taps_ref),
                ],
            )
            for copy in copies:
                copy.wait()


def swap(value, axis, distance):
    size = lax.axis_size(axis)
    return lax.ppermute(value, axis, [(i, i ^ distance) for i in range(size)])


def pause(value, received, mark):
    (mark,) = call(pause_body, [(mark.shape, F32)], value, mark, cost=1 << 36)
    return lax.optimization_barrier((received, mark))


def shards(features, couplings, neighbors, w_graph, kernel_taps, w_out, cotangent):
    bus, tm = lax.axis_size("bus"), lax.axis_size("tm")
    rows, steps, chans = features.shape
    blocks, slots, half = couplings.shape[:3]
    total = kernel_taps.shape[0]
    evens = [(i, i ^ 1) for i in range(bus)]
    odds = [(i, i + 1) for i in range(1, bus - 1, 2)] + [(i + 1, i) for i in range(1, bus - 1, 2)]
    odds += [(0, 0), (bus - 1, bus - 1)]
    wide = (steps, rows, chans)
    edge = (steps, half, chans)
    square = (chans, chans)

    def edge_of(even):
        (found,) = call(
            functools.partial(edge_body, even), [(edge, BF)], features,
            scratch=[
                pltpu.VMEM((half,) + features.shape[1:], BF), pltpu.SemaphoreType.DMA((half // 16,))
            ],
            far=[0],
        )
        return found

    even_own, odd_own = edge_of(True), edge_of(False)
    near = swap(cotangent, "tm", 1)
    odd_edge = lax.ppermute(odd_own, "bus", odds)
    even_edge = lax.ppermute(even_own, "bus", evens)
    far = swap(cotangent, "tm", 2)

    pairs = total // 2
    crossing = (pairs, chans, 2 * rows)
    ext = rows + 2 * half
    part = pltpu.VMEM((steps // 2, chans, 2 * rows), BF)
    sums, crossed, mix, mixt, steady, taps, wout, wg, lags = call(
        early_body,
        [
            (wide, F32), (crossing, BF), ((rows, ext), BF), ((ext, rows), BF), (wide, BF),
            (kernel_taps.shape, BF), (square, BF), (square, BF), ((total, 8, chans), F32),
        ],
        neighbors, couplings, cotangent, kernel_taps, w_out, w_graph, near,
        scratch=[
            part, pltpu.VMEM(wide, BF), pltpu.VMEM(wide, BF), part, pltpu.VMEM(wide, BF),
            pltpu.VMEM((blocks, blocks + 2, half, half), F32),
            pltpu.VMEM(couplings.shape, BF),
            pltpu.VMEM(cotangent.shape, BF),
            pltpu.SMEM(neighbors.shape, jnp.int32),
            pltpu.SemaphoreType.DMA((8,)),
        ],
        far=range(6), kept=(None, 1),
    )

    far, sums = lax.optimization_barrier((far, sums))
    swapped = swap(far, "tm", 1)
    sums, crossed = call(
        far_body, [(wide, F32), (crossing, BF)], sums, crossed, far, lags, wout,
        scratch=[
            pltpu.VMEM(wide, BF), part, pltpu.VMEM(wide, BF), pltpu.SemaphoreType.DMA((1,))
        ],
        kept=(1, 1),
    )
    even_edge, odd_edge, sums = lax.optimization_barrier((even_edge, odd_edge, sums))
    (mark,) = call(mark_body, [((8, chans), F32)], even_edge, odd_edge, cost=1 << 36)
    swapped, mark = lax.optimization_barrier((swapped, mark))
    size = (2 * chans + total) // 2
    keep, send, grad_mixed, even_grad, odd_grad = call(
        tail_body,
        [((size, chans), F32), ((size, chans), F32), (wide, BF), (edge, BF), (edge, BF)],
        even_own, odd_own, even_edge, odd_edge, mix, mixt, wg, wout, taps, lags,
        sums, swapped, crossed, mark,
        scratch=[
            pltpu.VMEM(wide, F32), pltpu.VMEM(wide, BF),
            pltpu.VMEM((steps // 2 + 1, 2 * rows, 2 * chans), BF),
            pltpu.VMEM(wide, BF), pltpu.VMEM(wide, BF), pltpu.VMEM(crossing, BF),
            pltpu.VMEM((32, 8, chans), F32), pltpu.VMEM(wide, BF),
            pltpu.VMEM((2 * size, chans), F32), pltpu.SemaphoreType.DMA((3,)),
        ],
        anywhere=[12],
    )
    mark = send[0:8]
    odd_grad = lax.ppermute(odd_grad, "bus", evens)
    keep = keep + swap(send, "tm", 1)
    keep, even_grad = lax.optimization_barrier((keep, even_grad))
    even_grad = lax.ppermute(even_grad, "bus", evens)
    hops = [("bus", 1 << bit) for bit in range(1, bus.bit_length() - 1)]
    hops += [("tm", 1 << bit) for bit in range(1, tm.bit_length() - 1)] + [("bus", 1)]
    onward = [(i, i + 2) for i in range(0, bus - 2, 2)] + [(i, i - 2) for i in range(3, bus, 2)]
    for place, (axis, distance) in enumerate(hops):
        sent = keep.astype(BF)
        received = swap(sent, axis, distance)
        if place < len(hops) - 2:
            received, mark = pause(keep, received, mark)
            if place == 0:
                odd_grad, mark = lax.optimization_barrier((odd_grad, mark))
                odd_grad = lax.ppermute(odd_grad, "bus", onward)
        elif place == len(hops) - 2:
            (spread,) = call(
                fold_body, [(wide, F32)], grad_mixed, mixt, steady, cost=1 << 36
            )
            received, spread = lax.optimization_barrier((received, spread))
        else:
            (spread,) = call(edge_add_body, [(wide, F32)], spread, even_grad, cost=1 << 36)
            received, spread = lax.optimization_barrier((received, spread))
        keep = sent.astype(F32) + received.astype(F32)
    keep = keep * (1.0 / math.sqrt(bus * rows * steps * tm))
    other = swap(keep, "tm", 1)
    (grad_features,) = call(
        final_body, [(features.shape, BF)], spread, odd_grad, cost=1 << 36
    )
    other, grad_features = lax.optimization_barrier((other, grad_features))
    grad_graph, grad_out, grad_taps = call(
        finish_body,
        [(square, F32), (square, F32), ((total, chans), F32)],
        keep, other, mark,
        scratch=[pltpu.SemaphoreType.DMA((4,))], placed=False,
    )
    return grad_features, grad_graph, grad_out, grad_taps


def solution(mesh):
    return jax.shard_map(
        shards,
        mesh=mesh,
        in_specs=(
            P("bus", "tm", None),
            P("bus", None, None, None),
            P("bus", None),
            P(),
            P(),
            P(),
            P("bus", "tm", None),
        ),
        out_specs=(P("bus", "tm", None), P(), P(), P()),
        check_vma=False,
    )
```
